256 devices in a mesh: frame: 16 (over z_hi, x, core), within: 16 (over y, z_lo).
Axes of the slice: x: 4, y: 4, z: 8 (z_hi: 2, z_lo: 4; z = z_hi * 4 + z_lo), core: 2. Of those that a mesh axis runs over, the one named last changes fastest.
Arguments:
- queries: bfloat16 [16, 1152, 1024], P('frame', 'within'), may hold values from -6 to 6
- keys_in: bfloat16 [16, 1152, 1024], P('frame', 'within'), may hold values from -6 to 6
- values_in: bfloat16 [16, 1152, 1024], P('frame', 'within'), may hold values from -6 to 6
- grad_out: bfloat16 [16, 1152, 1024], P('frame', 'within'), may hold values from -6 to 6
- partners: int32 [16, 2], replicated, may hold values from 0 to 15
- registers: int32 [16], replicated, may hold values from 1 to 288
Outputs:
- grad_queries: bfloat16 [16, 1152, 1024], P('frame', 'within')
- grad_keys: bfloat16 [16, 1152, 1024], P('frame', 'within')
- grad_values: bfloat16 [16, 1152, 1024], P('frame', 'within')
The draws below stay inside these ranges and needn't reach their ends.
Inputs may be any that keep to these rules, and one draw needn't show every extreme that they name: `partners`: A row may list a group more than once, and may list its own group.
All inputs are finite; a program needn't handle non-finite values.
Results may differ from the reference program's by a relative error of at most 0.012.
Values may be sent and summed in bfloat16 or wider, within the bound.
No kernel may reach another device: no remote copies, remote signals or barrier semaphores. Data moves between devices by JAX's collectives and lax.ppermute only.
A program may use at most 128 MiB of HBM per device.

```python
import math
import jax
import jax.numpy as jnp
import numpy as np
from jax import lax

HEADS = 16
DH = 64
D = 1024
PART = 2
G = 16
S = 1152


def draw_queries(key, part):
    base = jnp.clip(jax.random.normal(jax.random.fold_in(key, 1), (G, S, D), jnp.float32), -6.0, 6.0)
    return base.astype(jnp.bfloat16)


def draw_keys_in(key, part):
    base = jnp.clip(jax.random.normal(jax.random.fold_in(key, 2), (G, S, D), jnp.float32), -6.0, 6.0)
    return base.astype(jnp.bfloat16)


def set_ends(entries, own_key, least, top_value):
    shape = entries.shape
    place = [jax.random.randint(jax.random.fold_in(own_key, axis), (), 0, shape[axis]) for axis in range(len(shape))]
    entries = entries.at[tuple(place)].set(least)
    longest = shape.index(max(shape))
    place[longest] = (place[longest] + 1) % shape[longest]
    return entries.at[tuple(place)].set(top_value)


def block_scale(own_key, shape, pieces, low, high):
    def one(position, shards_of):
        steps = jax.random.uniform(jax.random.fold_in(jax.random.fold_in(own_key, 6), position), (shards_of,), jnp.float32, low / len(pieces), high / len(pieces))
        return jnp.repeat(jnp.exp(steps), shape[position] // shards_of).reshape((-1,) + (1,) * (len(shape) - position - 1))

    factor_of = one(*pieces[0])
    for cut in pieces[1:]:
        factor_of = factor_of * one(*cut)
    return factor_of


def cumulative_ranks(amount, slope):
    portions = [(1 << 20) // math.isqrt(rank ** slope) + 1 for rank in range(1, amount + 1)]
    scale = 1 + sum(portions) // (1 << 30)
    return np.cumsum(np.array([max(1, weight // scale) for weight in portions]))


def ranked_ids(stream_key, shape, count, skew):
    table = cumulative_ranks(count, skew)
    pick = jax.random.randint(jax.random.fold_in(stream_key, 1), shape, 0, int(table[count - 1]))
    rank = jnp.searchsorted(jnp.asarray(table, jnp.int32), pick, side="right")
    return jax.random.permutation(jax.random.fold_in(stream_key, 2), count)[rank].astype(jnp.int32)


def normal_values(stream_key, dims, spread, bound, pieces=(), held_as=jnp.bfloat16):
    gain = block_scale(stream_key, dims, pieces, -0.22, 0.18) if pieces else 1.0
    drawn = jax.random.normal(stream_key, dims, jnp.float32) * spread * gain
    return jnp.minimum(jnp.maximum(drawn, -bound), bound).astype(held_as)


def setup_inputs(seed: int = 0) -> dict:
    arg_keys = jax.random.split(jax.random.key(seed), 7)
    queries = draw_queries(jax.random.fold_in(arg_keys[6], 71), 0)
    keys_in = draw_keys_in(jax.random.fold_in(arg_keys[6], 71), 0)
    values_in = normal_values(arg_keys[2], (G, S, D), 1.0, 6.0, ((0, 16), (1, 16)))
    grad_out = normal_values(arg_keys[3], (G, S, D), 1.0, 6.0, ((0, 16), (1, 16)))
    partners = set_ends(ranked_ids(arg_keys[4], (G, PART), G, 2), jax.random.fold_in(arg_keys[4], 3), 0, G - 1).astype(jnp.int32)
    registers = set_ends(jax.random.randint(arg_keys[5], (G,), 1, S // 4 + 1), jax.random.fold_in(arg_keys[5], 1), 1, (S // 4 + 1) - 1).astype(jnp.int32)
    return dict(queries=queries, keys_in=keys_in, values_in=values_in, grad_out=grad_out, partners=partners, registers=registers)


def reference(queries, keys_in, values_in, grad_out, partners, registers):
    groups, seq, width = queries.shape
    scale = DH ** -0.5
    positions = jnp.arange(seq).astype(jnp.int32)

    def head_split(block):
        return block.reshape(block.shape[0], HEADS, DH).transpose(1, 0, 2)

    def one_head(operands):
        qh, kh, vh, dh, visible = operands
        raw = jnp.dot(qh, kh.T, preferred_element_type=jnp.float32) * scale
        raw = jnp.where(visible[None, :], raw, -1e30)
        top = jnp.max(raw, axis=1, keepdims=True)
        expo = jnp.exp(raw - top)
        prob = expo / jnp.sum(expo, axis=1, keepdims=True)
        dprod = jnp.dot(dh, vh.T, preferred_element_type=jnp.float32)
        delta = jnp.sum(prob * dprod, axis=1, keepdims=True)
        dscore = prob * (dprod - delta)
        prob_low = prob.astype(jnp.bfloat16)
        dscore_low = dscore.astype(jnp.bfloat16)
        dq = jnp.dot(dscore_low, kh, preferred_element_type=jnp.float32) * scale
        dk = jnp.dot(dscore_low.T, qh, preferred_element_type=jnp.float32) * scale
        dv = jnp.dot(prob_low.T, dh, preferred_element_type=jnp.float32)
        return dq, dk, dv

    def one_group(carry, index):
        dk_all, dv_all = carry
        listed = jnp.concatenate([index[None].astype(jnp.int32), partners[index].astype(jnp.int32)])
        keys_list = keys_in[listed].reshape(-1, width)
        values_list = values_in[listed].reshape(-1, width)
        hidden_regs = positions[None, :] >= registers[partners[index]][:, None]
        visible = jnp.concatenate([jnp.ones((seq,), dtype=bool), hidden_regs.reshape(-1)])
        visible_all = jnp.broadcast_to(visible[None, :], (HEADS, visible.shape[0]))
        dq, dk, dv = lax.map(one_head, (head_split(queries[index]), head_split(keys_list),
                                        head_split(values_list), head_split(grad_out[index]), visible_all))
        dq = dq.transpose(1, 0, 2).reshape(seq, width)
        dk = dk.transpose(1, 0, 2).reshape(PART + 1, seq, width)
        dv = dv.transpose(1, 0, 2).reshape(PART + 1, seq, width)
        dk_all = dk_all.at[listed].add(dk)
        dv_all = dv_all.at[listed].add(dv)
        return (dk_all, dv_all), dq.astype(jnp.bfloat16)

    start = (jnp.zeros((groups, seq, width), jnp.float32), jnp.zeros((groups, seq, width), jnp.float32))
    (dk_all, dv_all), grad_queries = lax.scan(one_group, start, jnp.arange(groups).astype(jnp.int32))
    return grad_queries, dk_all.astype(jnp.bfloat16), dv_all.astype(jnp.bfloat16)
```

```python
import jax
import jax.numpy as jnp
from jax import lax
from jax.experimental import pallas as pl
from jax.experimental.pallas import tpu as pltpu
from jax.sharding import PartitionSpec as P

DH = 64
HIDDEN_MOST = 288
BF16 = jnp.bfloat16
F32 = jnp.float32
VMEM = pl.BlockSpec(memory_space=pltpu.VMEM)
SMEM = pl.BlockSpec(memory_space=pltpu.SMEM)


def pair_up(low, high):
    return jnp.concatenate([low, high], axis=1)


def pack_kernel(q_ref, d_ref, k_ref, v_ref, out_ref):
    for pair in range(q_ref.shape[1] // (2 * DH)):
        cols = slice(2 * DH * pair, 2 * DH * (pair + 1))
        for place, (one, two) in enumerate(((q_ref, d_ref), (k_ref, v_ref))):
            a, b = one[:, cols], two[:, cols]
            lanes = slice(2 * DH * place, 2 * DH * (place + 1))
            out_ref[2 * pair, :, lanes] = pair_up(a[:, :DH], b[:, :DH])
            out_ref[2 * pair + 1, :, lanes] = pair_up(a[:, DH:], b[:, DH:])


def unpack_kernel(in_ref, q_ref, k_ref, v_ref):
    for pair in range(q_ref.shape[1] // (2 * DH)):
        cols = slice(2 * DH * pair, 2 * DH * (pair + 1))
        for place, out in enumerate((k_ref, v_ref, q_ref)):
            lanes = slice(DH * place, DH * (place + 1))
            out[:, cols] = pair_up(in_ref[2 * pair, :, lanes], in_ref[2 * pair + 1, :, lanes])


def pick_kernel(partners_ref, in_ref, out_ref):
    for group in range(in_ref.shape[0]):
        for slot in range(2):
            other = partners_ref[group, slot]
            out_ref[group, :, 128 * slot : 128 * (slot + 1)] = in_ref[other, :, 128:256]


def sum_kernel(partners_ref, own_ref, listed_ref, out_ref, total):
    groups = own_ref.shape[0]
    for group in range(groups):
        total[group] = own_ref[group, :, 0:128].astype(F32)
    for group in range(groups):
        for slot in range(2):
            other = partners_ref[group, slot]
            total[other] += listed_ref[group, :, 128 * slot : 128 * (slot + 1)].astype(F32)
    for group in range(groups):
        out_ref[group, :, 0:128] = total[group].astype(BF16)
        out_ref[group, :, 128:256] = own_ref[group, :, 128:256]


def attend_kernel(hidden_ref, own_ref, listed_ref, own_out, listed_out, kv, kt, s_ref, dp_ref, total):
    seq = own_ref.shape[0]
    kv[0] = own_ref[:, 128:256]
    kv[1] = listed_ref[:, 0:128]
    kv[2] = listed_ref[:, 128:256]
    for j in range(3):
        kt[j] = kv[j].T[:DH, :]
    total[...] = jnp.zeros_like(total)

    def tile(start, size):
        rows = pl.ds(start, size)
        qd = own_ref[rows, 0:128]
        left = lax.broadcasted_iota(jnp.int32, qd.shape, 1) < DH
        q_only = jnp.where(left, qd.astype(F32) * 0.125, 0.0).astype(BF16)
        d_only = jnp.where(left, 0.0, qd.astype(F32)).astype(BF16)
        nt = (((1,), (1,)), ((), ()))
        top = jnp.full((1, size), -jnp.inf, F32)
        for j in range(3):
            raw = lax.dot_general(kv[j], q_only, nt, preferred_element_type=F32)
            if j:
                head = raw[:HIDDEN_MOST]
                place = lax.broadcasted_iota(jnp.int32, head.shape, 0)
                head = jnp.where(place >= hidden_ref[j - 1], head, -1e30)
                raw = jnp.concatenate([head, raw[HIDDEN_MOST:]], axis=0)
            s_ref[j, :, :size] = raw
            top = jnp.maximum(top, jnp.max(raw, axis=0, keepdims=True))
        norm = jnp.zeros((1, size), F32)
        dsum = jnp.zeros((1, size), F32)
        for j in range(3):
            expo = jnp.exp(s_ref[j, :, :size] - top)
            dprod = lax.dot_general(kv[j], d_only, nt, preferred_element_type=F32)
            s_ref[j, :, :size] = expo
            dp_ref[j, :, :size] = dprod
            norm += jnp.sum(expo, axis=0, keepdims=True)
            dsum += jnp.sum(expo * dprod, axis=0, keepdims=True)
        inv = 1.0 / norm
        delta = dsum * inv
        dq = jnp.zeros((DH, size), F32)
        for j in range(3):
            prob = s_ref[j, :, :size] * inv
            dscore = (prob * (dp_ref[j, :, :size] - delta)).astype(BF16)
            prob = prob.astype(BF16)
            total[j] += jnp.dot(dscore, q_only, preferred_element_type=F32) + jnp.dot(
                prob, d_only, preferred_element_type=F32
            )
            dq += jnp.dot(kt[j], dscore, preferred_element_type=F32)
        dq = (dq * 0.125).T
        own_out[rows, 128:256] = pair_up(dq, jnp.zeros_like(dq)).astype(BF16)

    wide = 256

    @pl.loop(0, seq // wide)
    def _(i):
        tile(pl.multiple_of(i * wide, wide), wide)

    if seq % wide:
        tile(seq // wide * wide, seq % wide)
    own_out[:, 0:128] = total[0].astype(BF16)
    listed_out[:, 0:128] = total[1].astype(BF16)
    listed_out[:, 128:256] = total[2].astype(BF16)


def shape(*dims):
    return jax.ShapeDtypeStruct(dims, BF16)


def attend(hidden, own, listed):
    seq = own.shape[0]
    return pl.pallas_call(
        attend_kernel,
        out_shape=(shape(seq, 256), shape(seq, 256)),
        in_specs=[SMEM, VMEM, VMEM],
        out_specs=(VMEM, VMEM),
        scratch_shapes=[
            pltpu.VMEM((3, seq, 128), BF16),
            pltpu.VMEM((3, DH, seq), BF16),
            pltpu.VMEM((3, seq, 256), F32),
            pltpu.VMEM((3, seq, 256), F32),
            pltpu.VMEM((3, seq, 128), F32),
        ],
        compiler_params=pltpu.CompilerParams(vmem_limit_bytes=48 * 2**20),
        cost_estimate=pl.CostEstimate(flops=2 * 15 * seq * seq * DH, bytes_accessed=4 * seq * 512, transcendentals=3 * seq * seq),
        name="attend",
    )(hidden, own, listed)


def local(queries, keys_in, values_in, grad_out, partners, registers):
    rows, width = queries.shape[1:]
    heads = width // DH
    groups = partners.shape[0]
    small = pltpu.CompilerParams(vmem_limit_bytes=32 * 2**20)
    packed = pl.pallas_call(
        pack_kernel, out_shape=shape(heads, rows, 256), in_specs=[VMEM] * 4, out_specs=VMEM, name="pack", compiler_params=small
    )(queries[0], grad_out[0], keys_in[0], values_in[0])
    by_group = lax.all_to_all(packed, "frame", 0, 0, tiled=True)
    picked = pl.pallas_call(
        pick_kernel, out_shape=shape(groups, rows, 256), in_specs=[SMEM, VMEM], out_specs=VMEM, name="pick", compiler_params=small
    )(partners, by_group)
    own = lax.all_to_all(by_group, "within", 0, 0, tiled=True)
    listed = lax.all_to_all(picked, "within", 0, 0, tiled=True)
    hidden = registers[partners[lax.axis_index("within")]]
    seq = rows * own.shape[0]
    own_out, listed_out = attend(hidden, own.reshape(seq, 256), listed.reshape(seq, 256))
    own_out = lax.all_to_all(own_out.reshape(own.shape), "within", 0, 0, tiled=True)
    listed_out = lax.all_to_all(listed_out.reshape(own.shape), "within", 0, 0, tiled=True)
    summed = pl.pallas_call(
        sum_kernel,
        out_shape=shape(groups, rows, 256),
        in_specs=[SMEM, VMEM, VMEM],
        out_specs=VMEM,
        scratch_shapes=[pltpu.VMEM((groups, rows, 128), F32)],
        name="sum",
        compiler_params=small,
    )(partners, own_out, listed_out)
    by_head = lax.all_to_all(summed, "frame", 0, 0, tiled=True)
    dq, dk, dv = pl.pallas_call(
        unpack_kernel, out_shape=(shape(rows, width),) * 3, in_specs=[VMEM], out_specs=(VMEM,) * 3, name="unpack", compiler_params=small
    )(by_head)
    return dq[None], dk[None], dv[None]


def solution(mesh):
    tokens = P("frame", "within", None)
    return jax.shard_map(
        local,
        mesh=mesh,
        in_specs=(tokens,) * 4 + (P(), P()),
        out_specs=(tokens,) * 3,
        check_vma=False,
    )
```

```python
import jax
import jax.numpy as jnp
import numpy as np
from jax import lax
from jax.experimental import pallas as pl
from jax.experimental.pallas import tpu as pltpu
from jax.sharding import Mesh
from jax.sharding import PartitionSpec as P

DH = 64
HALF = DH // 2
HIDDEN_MOST = 288
BF16 = jnp.bfloat16
F32 = jnp.float32
VMEM = pl.BlockSpec(memory_space=pltpu.VMEM)
SMEM = pl.BlockSpec(memory_space=pltpu.SMEM)

FINE = (("zh", 2), ("x1", 2), ("x0", 2), ("c", 2), ("y", 4), ("zl1", 2), ("zl0", 2))
OUTER = ("zh", "x1", "x0", "c", "zl1")
INNER = ("y", "x0", "zl0")


def piece(head, half):
    return head // 4 * 8 + half * 4 + head % 4


def columns(head, half):
    return slice(DH * head + HALF * half, DH * head + HALF * (half + 1))


def pack_kernel(q_ref, d_ref, k_ref, v_ref, out_ref):
    for head in range(q_ref.shape[1] // DH):
        for half in range(2):
            parts = [ref[:, columns(head, half)] for ref in (q_ref, d_ref, k_ref, v_ref)]
            out_ref[piece(head, half)] = jnp.concatenate(parts, axis=1)


def unpack_kernel(in_ref, q_ref, k_ref, v_ref):
    for pair in range(q_ref.shape[1] // (2 * DH)):
        for out, place in ((q_ref, 0), (k_ref, 2), (v_ref, 3)):
            lanes = slice(HALF * place, HALF * (place + 1))
            parts = [in_ref[piece(2 * pair + i // 2, i % 2)][:, lanes] for i in range(4)]
            out[:, 2 * DH * pair : 2 * DH * (pair + 1)] = jnp.concatenate(parts, axis=1)


def pick_kernel(partners_ref, in_ref, out_ref):
    for group in range(in_ref.shape[0]):
        out_ref[group, :, 0:128] = in_ref[group]
        one, two = in_ref[partners_ref[group, 0]], in_ref[partners_ref[group, 1]]
        out_ref[group, :, 128:256] = jnp.concatenate([one[:, DH:], two[:, DH:]], axis=1)


def sum_kernel(partners_ref, in_ref, out_ref, total):
    groups = in_ref.shape[0]
    for group in range(groups):
        total[group] = in_ref[group, :, 0:128].astype(F32)
    left = lax.broadcasted_iota(jnp.int32, total.shape[1:], 1) < DH
    for group in range(groups):
        listed = in_ref[group, :, 128:256].astype(F32)
        one, two = partners_ref[group, 0], partners_ref[group, 1]
        total[one] += jnp.where(left, 0.0, pltpu.roll(listed, DH, 1))
        total[two] += jnp.where(left, 0.0, listed)
    for group in range(groups):
        out_ref[group] = total[group].astype(BF16)


WIDE = 256


def attend_kernel(hidden_ref, in_ref, out_ref, own, listed, kt, bias, s_ref, dp_ref, total):
    sources, rows_of = in_ref.shape[:2]
    seq = own.shape[0]
    blocks = [(s // 4 * 2 + s % 2, s // 2 % 2) for s in range(sources)]
    for source, (block, half) in enumerate(blocks):
        rows = slice(block * rows_of, (block + 1) * rows_of)
        lanes = slice(128 * half, 128 * (half + 1))
        own[rows, lanes] = in_ref[source, :, 0:128]
        listed[rows, lanes] = in_ref[source, :, 128:256]
    for j, (keys, place) in enumerate(((own, DH), (listed, 0), (listed, DH))):
        both = keys[...].T
        kt[j] = jnp.concatenate([both[place : place + HALF], both[128 + place : 128 + place + HALF]], axis=0)
    index = lax.broadcasted_iota(jnp.int32, bias.shape[1:], 0)
    chunk = rows_of // 2
    swap = (index >= chunk) & (index < 3 * chunk)
    place = jnp.where(swap, jnp.where(index < 2 * chunk, index + chunk, index - chunk), index)
    for j in range(2):
        bias[j] = jnp.where(place >= hidden_ref[j], 0.0, -1e30)
    total[...] = jnp.zeros_like(total)
    nt = (((1,), (1,)), ((), ()))

    def tile(start, size):
        rows = pl.ds(start, size)
        x = own[rows, :].astype(F32)
        lane = lax.broadcasted_iota(jnp.int32, x.shape, 1) % 128
        turned = jnp.concatenate([pltpu.roll(x[:, :128], DH, 1), pltpu.roll(x[:, 128:], DH, 1)], axis=1)
        q_low = jnp.where(lane < HALF, x * 0.125, 0.0).astype(BF16)
        d_low = jnp.where((lane >= HALF) & (lane < DH), x, 0.0).astype(BF16)
        q_high = jnp.where((lane >= DH) & (lane < DH + HALF), turned * 0.125, 0.0).astype(BF16)
        d_high = jnp.where(lane >= DH + HALF, turned, 0.0).astype(BF16)
        terms = ((own, q_high, d_high), (listed, q_low, d_low), (listed, q_high, d_high))
        top = jnp.full((1, size), -jnp.inf, F32)
        for j, (keys, q_side, _) in enumerate(terms):
            raw = lax.dot_general(keys[...], q_side, nt, preferred_element_type=F32)
            if j:
                head = raw[:HIDDEN_MOST] + bias[j - 1, :, :size]
                raw = jnp.concatenate([head, raw[HIDDEN_MOST:]], axis=0)
            s_ref[j, :, :size] = raw
            top = jnp.maximum(top, jnp.max(raw, axis=0, keepdims=True))
        norm = jnp.zeros((1, size), F32)
        dsum = jnp.zeros((1, size), F32)
        for j, (keys, _, d_side) in enumerate(terms):
            expo = jnp.exp(s_ref[j, :, :size] - top)
            dprod = lax.dot_general(keys[...], d_side, nt, preferred_element_type=F32)
            s_ref[j, :, :size] = expo
            dp_ref[j, :, :size] = dprod
            norm += jnp.sum(expo, axis=0, keepdims=True)
            dsum += jnp.sum(expo * dprod, axis=0, keepdims=True)
        inv = 1.0 / norm
        delta = dsum * inv
        dq = jnp.zeros((DH, size), F32)
        for j, (_, q_side, d_side) in enumerate(terms):
            prob = s_ref[j, :, :size] * inv
            dscore = (prob * (dp_ref[j, :, :size] - delta)).astype(BF16)
            both = jnp.concatenate([dscore, prob.astype(BF16)], axis=1)
            sides = jnp.concatenate([q_side, d_side], axis=0)
            total[min(j, 1)] += jnp.dot(both, sides, preferred_element_type=F32)
            dq += jnp.dot(kt[j], dscore, preferred_element_type=F32)
        dq = dq * 0.125
        gap = jnp.zeros((128 - HALF, size), F32)
        total[0, rows, :] += jnp.concatenate([dq[:HALF], gap, dq[HALF:], gap], axis=0).T

    @pl.loop(0, seq // WIDE)
    def _(i):
        tile(pl.multiple_of(i * WIDE, WIDE), WIDE)

    if seq % WIDE:
        tile(seq // WIDE * WIDE, seq % WIDE)
    for source, (block, half) in enumerate(blocks):
        rows = slice(block * rows_of, (block + 1) * rows_of)
        lanes = slice(128 * half, 128 * (half + 1))
        out_ref[source, :, 0:128] = total[0, rows, lanes].astype(BF16)
        out_ref[source, :, 128:256] = total[1, rows, lanes].astype(BF16)


def shape(*dims):
    return jax.ShapeDtypeStruct(dims, BF16)


def attend(hidden, rows):
    seq = rows.shape[0] * rows.shape[1] // 2
    return pl.pallas_call(
        attend_kernel,
        out_shape=shape(*rows.shape),
        in_specs=[SMEM, VMEM],
        out_specs=VMEM,
        scratch_shapes=[
            pltpu.VMEM((seq, 256), BF16),
            pltpu.VMEM((seq, 256), BF16),
            pltpu.VMEM((3, DH, seq), BF16),
            pltpu.VMEM((2, HIDDEN_MOST, WIDE), F32),
            pltpu.VMEM((3, seq, WIDE), F32),
            pltpu.VMEM((3, seq, WIDE), F32),
            pltpu.VMEM((2, seq, 256), F32),
        ],
        compiler_params=pltpu.CompilerParams(vmem_limit_bytes=48 * 2**20),
        name="attend",
    )(hidden, rows)


def local(queries, keys_in, values_in, grad_out, partners, registers):
    rows, width = queries.shape[1:]
    groups = partners.shape[0]
    pieces = 2 * width // DH
    small = pltpu.CompilerParams(vmem_limit_bytes=32 * 2**20)
    packed = pl.pallas_call(
        pack_kernel, out_shape=shape(pieces, rows, 128), in_specs=[VMEM] * 4, out_specs=VMEM, name="pack", compiler_params=small
    )(queries[0], grad_out[0], keys_in[0], values_in[0])
    by_group = lax.all_to_all(packed, OUTER, 0, 0, tiled=True).reshape(groups, 2 * rows, 128)
    picked = pl.pallas_call(
        pick_kernel, out_shape=shape(groups, 2 * rows, 256), in_specs=[SMEM, VMEM], out_specs=VMEM, name="pick", compiler_params=small
    )(partners, by_group)
    gathered = lax.all_to_all(picked, INNER, 0, 0, tiled=True)
    hidden = registers[partners[lax.axis_index(INNER)]]
    spread = lax.all_to_all(attend(hidden, gathered), INNER, 0, 0, tiled=True)
    summed = pl.pallas_call(
        sum_kernel,
        out_shape=shape(groups, 2 * rows, 128),
        in_specs=[SMEM, VMEM],
        out_specs=VMEM,
        scratch_shapes=[pltpu.VMEM((groups, 2 * rows, 128), F32)],
        name="sum",
        compiler_params=small,
    )(partners, spread)
    by_head = lax.all_to_all(summed.reshape(pieces, rows, 128), OUTER, 0, 0, tiled=True)
    dq, dk, dv = pl.pallas_call(
        unpack_kernel, out_shape=(shape(rows, width),) * 3, in_specs=[VMEM], out_specs=(VMEM,) * 3, name="unpack", compiler_params=small
    )(by_head)
    return dq[None], dk[None], dv[None]


def solution(mesh):
    names = tuple(name for name, _ in FINE)
    fine = Mesh(np.asarray(mesh.devices).reshape([size for _, size in FINE]), names)
    tokens = P(names[:4], names[4:], None)
    return jax.shard_map(
        local,
        mesh=fine,
        in_specs=(tokens,) * 4 + (P(), P()),
        out_specs=(tokens,) * 3,
        check_vma=False,
    )
```

```python
import jax
import jax.numpy as jnp
import numpy as np
from jax import lax
from jax.experimental import pallas as pl
from jax.experimental.pallas import tpu as pltpu
from jax.sharding import Mesh
from jax.sharding import PartitionSpec as P

DH = 64
HALF = DH // 2
REST = 16
HIDDEN_MOST = 288
BF16 = jnp.bfloat16
F32 = jnp.float32
VMEM = pl.BlockSpec(memory_space=pltpu.VMEM)
HBM = pl.BlockSpec(memory_space=pltpu.HBM)
SMEM = pl.BlockSpec(memory_space=pltpu.SMEM)

FINE = (("zh", 2), ("x1", 2), ("x0", 2), ("c", 2), ("y", 4), ("zl1", 2), ("zl0", 2))
OUTER = ("zh", "x1", "x0", "c", "zl1")
INNER = ("y", "x0", "zl0")


def piece(head, half):
    return head // 4 * 8 + half * 4 + head % 4


def columns(head, half):
    return slice(DH * head + HALF * half, DH * head + HALF * (half + 1))


def pack_kernel(q_hbm, d_hbm, k_hbm, v_hbm, out_ref, q_ref, d_ref, k_ref, v_ref, sems):
    refs = (q_ref, d_ref, k_ref, v_ref)
    copies = [pltpu.make_async_copy(a, b, sems.at[i]) for i, (a, b) in enumerate(zip((q_hbm, d_hbm, k_hbm, v_hbm), refs))]
    for copy in copies:
        copy.start()
    for copy in copies:
        copy.wait()
    for head in range(q_ref.shape[1] // DH):
        for half in range(2):
            parts = [ref[:, columns(head, half)] for ref in refs]
            out_ref[piece(head, half)] = jnp.concatenate(parts, axis=1)


def unpack_kernel(in_ref, q_ref, k_ref, v_ref):
    def unfold(at):
        x = in_ref[at].astype(F32)
        lane = lax.broadcasted_iota(jnp.int32, (REST, 128), 1)
        q, k, v = (pltpu.roll(x[REST * i : REST * (i + 1)], shift, 1) for i, shift in enumerate((128 - HALF, HALF, 2 * HALF)))
        return jnp.concatenate([x, jnp.where(lane < HALF, q, jnp.where(lane < 3 * HALF, k, v))], axis=0)

    for pair in range(q_ref.shape[1] // (2 * DH)):
        parts = [unfold(piece(2 * pair + i // 2, i % 2)) for i in range(4)]
        lane = lax.broadcasted_iota(jnp.int32, parts[0].shape, 1)
        for out, place in ((q_ref, 0), (k_ref, 2), (v_ref, 3)):
            row = parts[place]
            for i in range(4):
                if i != place:
                    turned = pltpu.roll(parts[i], (HALF * (i - place)) % 128, 1)
                    row = jnp.where((lane >= HALF * i) & (lane < HALF * (i + 1)), turned, row)
            out[:, 2 * DH * pair : 2 * DH * (pair + 1)] = row.astype(BF16)


def pick_kernel(partners_ref, in_ref, out_ref):
    for group in range(in_ref.shape[0]):
        out_ref[group, :, 0:128] = in_ref[group]
        one, two = in_ref[partners_ref[group, 0]], in_ref[partners_ref[group, 1]]
        out_ref[group, :, 128:256] = jnp.concatenate([one[:, DH:], two[:, DH:]], axis=1)


def sum_kernel(partners_ref, in_ref, out_ref, total):
    groups = in_ref.shape[0]
    for group in range(groups):
        total[group] = in_ref[group, :, 0:128].astype(F32)
    left = lax.broadcasted_iota(jnp.int32, total.shape[1:], 1) < DH
    for group in range(groups):
        listed = in_ref[group, :, 128:256].astype(F32)
        one, two = partners_ref[group, 0], partners_ref[group, 1]
        total[one] += jnp.where(left, 0.0, pltpu.roll(listed, DH, 1))
        total[two] += jnp.where(left, 0.0, listed)
    folded = out_ref.shape[1]
    lane = lax.broadcasted_iota(jnp.int32, (folded, 128), 1)
    spare = (lane >= HALF) & (lane < DH)
    for group in range(groups):
        for chunk in range(2):
            x = total[group, chunk * (folded + REST) : (chunk + 1) * (folded + REST)]
            rest = x[folded:]
            fill = [pltpu.roll(rest, shift, 1) for shift in (HALF, 128 - HALF, 128 - 2 * HALF)]
            fill = jnp.concatenate(fill + [jnp.zeros((folded - 3 * REST, 128), F32)], axis=0)
            out_ref[2 * group + chunk] = jnp.where(spare, fill, x[:folded]).astype(BF16)


WIDE = 256


def attend_kernel(hidden_ref, in_ref, out_ref, own, listed, kt, bias, s_ref, dp_ref, total):
    sources, rows_of = in_ref.shape[:2]
    seq = own.shape[0]
    blocks = [(s // 4 * 2 + s % 2, s // 2 % 2) for s in range(sources)]
    for source, (block, half) in enumerate(blocks):
        rows = slice(block * rows_of, (block + 1) * rows_of)
        lanes = slice(128 * half, 128 * (half + 1))
        own[rows, lanes] = in_ref[source, :, 0:128]
        listed[rows, lanes] = in_ref[source, :, 128:256]
    for j, (keys, place) in enumerate(((own, DH), (listed, 0), (listed, DH))):
        both = keys[...].T
        kt[j] = jnp.concatenate([both[place : place + HALF], both[128 + place : 128 + place + HALF]], axis=0)
    index = lax.broadcasted_iota(jnp.int32, bias.shape[1:], 0)
    chunk = rows_of // 2
    swap = (index >= chunk) & (index < 3 * chunk)
    place = jnp.where(swap, jnp.where(index < 2 * chunk, index + chunk, index - chunk), index)
    for j in range(2):
        bias[j] = jnp.where(place >= hidden_ref[j], 0.0, -1e30)
    total[...] = jnp.zeros_like(total)
    nt = (((1,), (1,)), ((), ()))

    def tile(start, size):
        rows = pl.ds(start, size)
        x = own[rows, :].astype(F32)
        lane = lax.broadcasted_iota(jnp.int32, x.shape, 1) % 128
        turned = jnp.concatenate([pltpu.roll(x[:, :128], DH, 1), pltpu.roll(x[:, 128:], DH, 1)], axis=1)
        q_low = jnp.where(lane < HALF, x * 0.125, 0.0).astype(BF16)
        d_low = jnp.where((lane >= HALF) & (lane < DH), x, 0.0).astype(BF16)
        q_high = jnp.where((lane >= DH) & (lane < DH + HALF), turned * 0.125, 0.0).astype(BF16)
        d_high = jnp.where(lane >= DH + HALF, turned, 0.0).astype(BF16)
        terms = ((own, q_high, d_high), (listed, q_low, d_low), (listed, q_high, d_high))
        top = jnp.full((1, size), -jnp.inf, F32)
        for j, (keys, q_side, _) in enumerate(terms):
            raw = lax.dot_general(keys[...], q_side, nt, preferred_element_type=F32)
            if j:
                head = raw[:HIDDEN_MOST] + bias[j - 1, :, :size]
                raw = jnp.concatenate([head, raw[HIDDEN_MOST:]], axis=0)
            s_ref[j, :, :size] = raw
            top = jnp.maximum(top, jnp.max(raw, axis=0, keepdims=True))
        norm = jnp.zeros((1, size), F32)
        dsum = jnp.zeros((1, size), F32)
        for j, (keys, _, d_side) in enumerate(terms):
            expo = jnp.exp(s_ref[j, :, :size] - top)
            dprod = lax.dot_general(keys[...], d_side, nt, preferred_element_type=F32)
            s_ref[j, :, :size] = expo
            dp_ref[j, :, :size] = dprod
            norm += jnp.sum(expo, axis=0, keepdims=True)
            dsum += jnp.sum(expo * dprod, axis=0, keepdims=True)
        inv = 1.0 / norm
        delta = dsum * inv
        dq = jnp.zeros((DH, size), F32)
        for j, (_, q_side, d_side) in enumerate(terms):
            prob = s_ref[j, :, :size] * inv
            dscore = (prob * (dp_ref[j, :, :size] - delta)).astype(BF16)
            both = jnp.concatenate([dscore, prob.astype(BF16)], axis=1)
            sides = jnp.concatenate([q_side, d_side], axis=0)
            total[min(j, 1)] += jnp.dot(both, sides, preferred_element_type=F32)
            dq += jnp.dot(kt[j], dscore, preferred_element_type=F32)
        dq = dq * 0.125
        gap = jnp.zeros((128 - HALF, size), F32)
        total[0, rows, :] += jnp.concatenate([dq[:HALF], gap, dq[HALF:], gap], axis=0).T

    @pl.loop(0, seq // WIDE)
    def _(i):
        tile(pl.multiple_of(i * WIDE, WIDE), WIDE)

    if seq % WIDE:
        tile(seq // WIDE * WIDE, seq % WIDE)
    for source, (block, half) in enumerate(blocks):
        rows = slice(block * rows_of, (block + 1) * rows_of)
        lanes = slice(128 * half, 128 * (half + 1))
        out_ref[source, :, 0:128] = total[0, rows, lanes].astype(BF16)
        out_ref[source, :, 128:256] = total[1, rows, lanes].astype(BF16)


def shape(*dims):
    return jax.ShapeDtypeStruct(dims, BF16)


def attend(hidden, rows):
    seq = rows.shape[0] * rows.shape[1] // 2
    return pl.pallas_call(
        attend_kernel,
        out_shape=shape(*rows.shape),
        in_specs=[SMEM, VMEM],
        out_specs=VMEM,
        scratch_shapes=[
            pltpu.VMEM((seq, 256), BF16),
            pltpu.VMEM((seq, 256), BF16),
            pltpu.VMEM((3, DH, seq), BF16),
            pltpu.VMEM((2, HIDDEN_MOST, WIDE), F32),
            pltpu.VMEM((3, seq, WIDE), F32),
            pltpu.VMEM((3, seq, WIDE), F32),
            pltpu.VMEM((2, seq, 256), F32),
        ],
        compiler_params=pltpu.CompilerParams(vmem_limit_bytes=48 * 2**20),
        name="attend",
    )(hidden, rows)


def local(queries, keys_in, values_in, grad_out, partners, registers):
    rows, width = queries.shape[1:]
    groups = partners.shape[0]
    pieces = 2 * width // DH
    small = pltpu.CompilerParams(vmem_limit_bytes=32 * 2**20)
    packed = pl.pallas_call(
        pack_kernel, out_shape=shape(pieces, rows, 128), in_specs=[HBM] * 4, out_specs=VMEM, name="pack",
        compiler_params=pltpu.CompilerParams(vmem_limit_bytes=63_400_000),
        scratch_shapes=[pltpu.VMEM((rows, width), BF16)] * 4 + [pltpu.SemaphoreType.DMA((4,))],
    )(queries[0], grad_out[0], keys_in[0], values_in[0])
    by_group = lax.all_to_all(packed, OUTER, 0, 0, tiled=True).reshape(groups, 2 * rows, 128)
    picked = pl.pallas_call(
        pick_kernel, out_shape=shape(groups, 2 * rows, 256), in_specs=[SMEM, VMEM], out_specs=VMEM, name="pick", compiler_params=small
    )(partners, by_group)
    gathered = lax.all_to_all(picked, INNER, 0, 0, tiled=True)
    hidden = registers[partners[lax.axis_index(INNER)]]
    spread = lax.all_to_all(attend(hidden, gathered), INNER, 0, 0, tiled=True)
    summed = pl.pallas_call(
        sum_kernel,
        out_shape=shape(pieces, rows - REST, 128),
        in_specs=[SMEM, VMEM],
        out_specs=VMEM,
        scratch_shapes=[pltpu.VMEM((groups, 2 * rows, 128), F32)],
        name="sum",
        compiler_params=small,
    )(partners, spread)
    by_head = lax.all_to_all(summed, OUTER, 0, 0, tiled=True)
    dq, dk, dv = pl.pallas_call(
        unpack_kernel, out_shape=(shape(rows, width),) * 3, in_specs=[VMEM], out_specs=(VMEM,) * 3, name="unpack", compiler_params=small
    )(by_head)
    return dq[None], dk[None], dv[None]


def solution(mesh):
    names = tuple(name for name, _ in FINE)
    fine = Mesh(np.asarray(mesh.devices).reshape([size for _, size in FINE]), names)
    tokens = P(names[:4], names[4:], None)
    return jax.shard_map(
        local,
        mesh=fine,
        in_specs=(tokens,) * 4 + (P(), P()),
        out_specs=(tokens,) * 3,
        check_vma=False,
    )
```

```python
import jax
import jax.numpy as jnp
import numpy as np
from jax import lax
from jax.experimental import pallas as pl
from jax.experimental.pallas import tpu as pltpu
from jax.sharding import Mesh
from jax.sharding import PartitionSpec as P

DH = 64
HALF = DH // 2
REST = 16
HIDDEN_MOST = 288
BF16 = jnp.bfloat16
F32 = jnp.float32
VMEM = pl.BlockSpec(memory_space=pltpu.VMEM)
HBM = pl.BlockSpec(memory_space=pltpu.HBM)
SMEM = pl.BlockSpec(memory_space=pltpu.SMEM)

FINE = (("zh", 2), ("x1", 2), ("x0", 2), ("c", 2), ("y", 4), ("zl1", 2), ("zl0", 2))
OUTER = ("zh", "x1", "x0", "c", "zl1")
INNER = ("y", "x0", "zl0")


def piece(head, half):
    return head // 4 * 8 + half * 4 + head % 4


def columns(head, half):
    return slice(DH * head + HALF * half, DH * head + HALF * (half + 1))


def pack_kernel(q_hbm, d_hbm, k_hbm, v_hbm, out_ref, q_ref, d_ref, k_ref, v_ref, sems):
    refs = (q_ref, d_ref, k_ref, v_ref)
    copies = [pltpu.make_async_copy(a, b, sems.at[i]) for i, (a, b) in enumerate(zip((q_hbm, d_hbm, k_hbm, v_hbm), refs))]
    for copy in copies:
        copy.start()
    for copy in copies:
        copy.wait()
    for head in range(q_ref.shape[1] // DH):
        for half in range(2):
            parts = [ref[:, columns(head, half)] for ref in refs]
            out_ref[piece(head, half)] = jnp.concatenate(parts, axis=1)


def unpack_kernel(in_ref, q_ref, k_ref, v_ref):
    def unfold(at):
        x = in_ref[at].astype(F32)
        lane = lax.broadcasted_iota(jnp.int32, (REST, 128), 1)
        q, k, v = (pltpu.roll(x[REST * i : REST * (i + 1)], shift, 1) for i, shift in enumerate((128 - HALF, HALF, 2 * HALF)))
        return jnp.concatenate([x, jnp.where(lane < HALF, q, jnp.where(lane < 3 * HALF, k, v))], axis=0)

    for pair in range(q_ref.shape[1] // (2 * DH)):
        parts = [unfold(piece(2 * pair + i // 2, i % 2)) for i in range(4)]
        lane = lax.broadcasted_iota(jnp.int32, parts[0].shape, 1)
        for out, place in ((q_ref, 0), (k_ref, 2), (v_ref, 3)):
            row = parts[place]
            for i in range(4):
                if i != place:
                    turned = pltpu.roll(parts[i], (HALF * (i - place)) % 128, 1)
                    row = jnp.where((lane >= HALF * i) & (lane < HALF * (i + 1)), turned, row)
            out[:, 2 * DH * pair : 2 * DH * (pair + 1)] = row.astype(BF16)


def pick_kernel(partners_ref, in_ref, out_ref):
    for group in range(in_ref.shape[0]):
        out_ref[group, :, 0:128] = in_ref[group]
        one, two = in_ref[partners_ref[group, 0]], in_ref[partners_ref[group, 1]]
        out_ref[group, :, 128:256] = jnp.concatenate([one[:, DH:], two[:, DH:]], axis=1)


def sum_kernel(partners_ref, in_ref, out_ref, total):
    groups = in_ref.shape[0]
    for group in range(groups):
        total[group] = in_ref[group, :, 0:128].astype(F32)
    left = lax.broadcasted_iota(jnp.int32, total.shape[1:], 1) < DH
    for group in range(groups):
        listed = in_ref[group, :, 128:256].astype(F32)
        one, two = partners_ref[group, 0], partners_ref[group, 1]
        total[one] += jnp.where(left, 0.0, pltpu.roll(listed, DH, 1))
        total[two] += jnp.where(left, 0.0, listed)
    folded = out_ref.shape[1]
    lane = lax.broadcasted_iota(jnp.int32, (folded, 128), 1)
    spare = (lane >= HALF) & (lane < DH)
    for group in range(groups):
        for chunk in range(2):
            x = total[group, chunk * (folded + REST) : (chunk + 1) * (folded + REST)]
            rest = x[folded:]
            fill = [pltpu.roll(rest, shift, 1) for shift in (HALF, 128 - HALF, 128 - 2 * HALF)]
            fill = jnp.concatenate(fill + [jnp.zeros((folded - 3 * REST, 128), F32)], axis=0)
            out_ref[2 * group + chunk] = jnp.where(spare, fill, x[:folded]).astype(BF16)


WIDE = 1152


def attend_kernel(hidden_ref, in_ref, out_ref, own, listed, kt, bias, s_ref, dp_ref, total, flat, dqt):
    sources, rows_of = in_ref.shape[:2]
    seq = own.shape[0]
    blocks = [(s // 4 * 2 + s % 2, s // 2 % 2) for s in range(sources)]
    for source, (block, half) in enumerate(blocks):
        rows = slice(block * rows_of, (block + 1) * rows_of)
        lanes = slice(128 * half, 128 * (half + 1))
        own[rows, lanes] = in_ref[source, :, 0:128]
        listed[rows, lanes] = in_ref[source, :, 128:256]
    flipped = (own[...].T, listed[...].T)
    both = lambda x, place: jnp.concatenate([x[place : place + HALF], x[128 + place : 128 + place + HALF]], axis=0)
    for j, (x, place) in enumerate(((flipped[0], DH), (flipped[1], 0), (flipped[1], DH))):
        kt[j] = both(x, place)
    flat[:DH] = (both(flipped[0], 0).astype(F32) * 0.125).astype(BF16)
    flat[DH:] = both(flipped[0], HALF)
    index = lax.broadcasted_iota(jnp.int32, bias.shape[1:], 0)
    chunk = rows_of // 2
    swap = (index >= chunk) & (index < 3 * chunk)
    place = jnp.where(swap, jnp.where(index < 2 * chunk, index + chunk, index - chunk), index)
    for j in range(2):
        bias[j] = jnp.where(place >= hidden_ref[j], 0.0, -1e30)
    total[...] = jnp.zeros_like(total)
    nt = (((1,), (1,)), ((), ()))

    def tile(start, size):
        rows = pl.ds(start, size)
        x = own[rows, :].astype(F32)
        lane = lax.broadcasted_iota(jnp.int32, x.shape, 1) % 128
        turned = jnp.concatenate([pltpu.roll(x[:, :128], DH, 1), pltpu.roll(x[:, 128:], DH, 1)], axis=1)
        q_low = jnp.where(lane < HALF, x * 0.125, 0.0).astype(BF16)
        d_low = jnp.where((lane >= HALF) & (lane < DH), x, 0.0).astype(BF16)
        q_high = jnp.where((lane >= DH) & (lane < DH + HALF), turned * 0.125, 0.0).astype(BF16)
        d_high = jnp.where(lane >= DH + HALF, turned, 0.0).astype(BF16)
        terms = ((own, q_high, d_high), (listed, q_low, d_low), (listed, q_high, d_high))
        top = jnp.full((1, size), -jnp.inf, F32)
        for j, (keys, q_side, _) in enumerate(terms):
            raw = lax.dot_general(keys[...], q_side, nt, preferred_element_type=F32)
            if j:
                head = raw[:HIDDEN_MOST] + bias[j - 1, :, :size]
                raw = jnp.concatenate([head, raw[HIDDEN_MOST:]], axis=0)
            s_ref[j, :, :size] = raw
            top = jnp.maximum(top, jnp.max(raw, axis=0, keepdims=True))
        norm = jnp.zeros((1, size), F32)
        dsum = jnp.zeros((1, size), F32)
        for j, (keys, _, d_side) in enumerate(terms):
            expo = jnp.exp(s_ref[j, :, :size] - top)
            dprod = lax.dot_general(keys[...], d_side, nt, preferred_element_type=F32)
            s_ref[j, :, :size] = expo
            dp_ref[j, :, :size] = dprod
            norm += jnp.sum(expo, axis=0, keepdims=True)
            dsum += jnp.sum(expo * dprod, axis=0, keepdims=True)
        inv = 1.0 / norm
        delta = dsum * inv
        dq = jnp.zeros((DH, size), F32)
        for j, (_, q_side, d_side) in enumerate(terms):
            prob = s_ref[j, :, :size] * inv
            dscore = (prob * (dp_ref[j, :, :size] - delta)).astype(BF16)
            total[j, :DH] += lax.dot_general(flat[:DH, rows], dscore, nt, preferred_element_type=F32)
            total[j, DH:] += lax.dot_general(flat[DH:, rows], prob.astype(BF16), nt, preferred_element_type=F32)
            dq += jnp.dot(kt[j], dscore, preferred_element_type=F32)
        dqt[:, rows] = dq

    @pl.loop(0, seq // WIDE)
    def _(i):
        tile(pl.multiple_of(i * WIDE, WIDE), WIDE)

    if seq % WIDE:
        tile(seq // WIDE * WIDE, seq % WIDE)
    gap = jnp.zeros((HALF, seq), F32)
    for half in range(2):
        part = slice(HALF * half, HALF * (half + 1))
        value = slice(DH + HALF * half, DH + HALF * (half + 1))
        own_part = jnp.concatenate([dqt[part] * 0.125, gap, total[0, part], total[0, value]], axis=0).T.astype(BF16)
        listed_part = jnp.concatenate([total[1, part], total[1, value], total[2, part], total[2, value]], axis=0).T.astype(BF16)
        for source, (block, which) in enumerate(blocks):
            if which == half:
                rows = slice(block * rows_of, (block + 1) * rows_of)
                out_ref[source, :, 0:128] = own_part[rows]
                out_ref[source, :, 128:256] = listed_part[rows]


def shape(*dims):
    return jax.ShapeDtypeStruct(dims, BF16)


def attend(hidden, rows):
    seq = rows.shape[0] * rows.shape[1] // 2
    return pl.pallas_call(
        attend_kernel,
        out_shape=shape(*rows.shape),
        in_specs=[SMEM, VMEM],
        out_specs=VMEM,
        scratch_shapes=[
            pltpu.VMEM((seq, 256), BF16),
            pltpu.VMEM((seq, 256), BF16),
            pltpu.VMEM((3, DH, seq), BF16),
            pltpu.VMEM((2, HIDDEN_MOST, WIDE), F32),
            pltpu.VMEM((3, seq, WIDE), F32),
            pltpu.VMEM((3, seq, WIDE), F32),
            pltpu.VMEM((3, 2 * DH, seq), F32),
            pltpu.VMEM((2 * DH, seq), BF16),
            pltpu.VMEM((DH, seq), F32),
        ],
        compiler_params=pltpu.CompilerParams(vmem_limit_bytes=46 * 2**20),
        name="attend",
    )(hidden, rows)


def local(queries, keys_in, values_in, grad_out, partners, registers):
    rows, width = queries.shape[1:]
    groups = partners.shape[0]
    pieces = 2 * width // DH
    small = pltpu.CompilerParams(vmem_limit_bytes=32 * 2**20)
    packed = pl.pallas_call(
        pack_kernel, out_shape=shape(pieces, rows, 128), in_specs=[HBM] * 4, out_specs=VMEM, name="pack",
        compiler_params=pltpu.CompilerParams(vmem_limit_bytes=63_400_000),
        scratch_shapes=[pltpu.VMEM((rows, width), BF16)] * 4 + [pltpu.SemaphoreType.DMA((4,))],
    )(queries[0], grad_out[0], keys_in[0], values_in[0])
    by_group = lax.all_to_all(packed, OUTER, 0, 0, tiled=True).reshape(groups, 2 * rows, 128)
    picked = pl.pallas_call(
        pick_kernel, out_shape=shape(groups, 2 * rows, 256), in_specs=[SMEM, VMEM], out_specs=VMEM, name="pick", compiler_params=small
    )(partners, by_group)
    gathered = lax.all_to_all(picked, INNER, 0, 0, tiled=True)
    hidden = registers[partners[lax.axis_index(INNER)]]
    spread = lax.all_to_all(attend(hidden, gathered), INNER, 0, 0, tiled=True)
    summed = pl.pallas_call(
        sum_kernel,
        out_shape=shape(pieces, rows - REST, 128),
        in_specs=[SMEM, VMEM],
        out_specs=VMEM,
        scratch_shapes=[pltpu.VMEM((groups, 2 * rows, 128), F32)],
        name="sum",
        compiler_params=small,
    )(partners, spread)
    by_head = lax.all_to_all(summed, OUTER, 0, 0, tiled=True)
    dq, dk, dv = pl.pallas_call(
        unpack_kernel, out_shape=(shape(rows, width),) * 3, in_specs=[VMEM], out_specs=(VMEM,) * 3, name="unpack", compiler_params=small
    )(by_head)
    return dq[None], dk[None], dv[None]


def solution(mesh):
    names = tuple(name for name, _ in FINE)
    fine = Mesh(np.asarray(mesh.devices).reshape([size for _, size in FINE]), names)
    tokens = P(names[:4], names[4:], None)
    return jax.shard_map(
        local,
        mesh=fine,
        in_specs=(tokens,) * 4 + (P(), P()),
        out_specs=(tokens,) * 3,
        check_vma=False,
    )
```

```python
import jax
import jax.numpy as jnp
import numpy as np
from jax import lax
from jax.experimental import pallas as pl
from jax.experimental.pallas import tpu as pltpu
from jax.sharding import Mesh
from jax.sharding import PartitionSpec as P

DH = 64
HALF = DH // 2
REST = 16
HIDDEN_MOST = 288
BF16 = jnp.bfloat16
F32 = jnp.float32
VMEM = pl.BlockSpec(memory_space=pltpu.VMEM)
HBM = pl.BlockSpec(memory_space=pltpu.HBM)
SMEM = pl.BlockSpec(memory_space=pltpu.SMEM)

FINE = (("zh", 2), ("x1", 2), ("x0", 2), ("c", 2), ("y", 4), ("zl1", 2), ("zl0", 2))
OUTER = ("zh", "x1", "x0", "c", "zl1")
INNER = ("y", "x0", "zl0")


def piece(head, half):
    return head // 4 * 8 + half * 4 + head % 4


def columns(head, half):
    return slice(DH * head + HALF * half, DH * head + HALF * (half + 1))


def slots(rows):
    return lax.broadcasted_iota(jnp.int32, (rows, 128), 1) // HALF


def spare(rows):
    return slots(rows) == 1


def to_spare(x, slot):
    return x if slot == 1 else pltpu.roll(x, (HALF - HALF * slot) % 128, 1)


def from_spare(x, start, places):
    slot = slots(REST)
    out = jnp.zeros((REST, 128), F32)
    for i, place in enumerate(places):
        part = x[start + REST * i : start + REST * (i + 1)]
        part = part if place == 1 else pltpu.roll(part, (HALF * place - HALF) % 128, 1)
        out = jnp.where(slot == place, part, out)
    return out


def pack_kernel(q_hbm, d_hbm, k_hbm, v_hbm, out_ref, q_ref, d_ref, k_ref, v_ref, sems):
    refs = (q_ref, d_ref, k_ref, v_ref)
    copies = [pltpu.make_async_copy(a, b, sems.at[i]) for i, (a, b) in enumerate(zip((q_hbm, d_hbm, k_hbm, v_hbm), refs))]
    for copy in copies:
        copy.start()
    for copy in copies:
        copy.wait()
    for head in range(q_ref.shape[1] // DH):
        for half in range(2):
            parts = [ref[:, columns(head, half)] for ref in refs]
            out_ref[piece(head, half)] = jnp.concatenate(parts, axis=1)


def unpack_kernel(in_ref, q_ref, k_ref, v_ref):
    def unfold(at):
        x = in_ref[at].astype(F32)
        return jnp.concatenate([x, from_spare(x, 0, (0, 2, 3))], axis=0)

    for pair in range(q_ref.shape[1] // (2 * DH)):
        parts = [unfold(piece(2 * pair + i // 2, i % 2)) for i in range(4)]
        lane = lax.broadcasted_iota(jnp.int32, parts[0].shape, 1)
        for out, place in ((q_ref, 0), (k_ref, 2), (v_ref, 3)):
            row = parts[place]
            for i in range(4):
                if i != place:
                    turned = pltpu.roll(parts[i], (HALF * (i - place)) % 128, 1)
                    row = jnp.where((lane >= HALF * i) & (lane < HALF * (i + 1)), turned, row)
            out[:, 2 * DH * pair : 2 * DH * (pair + 1)] = row.astype(BF16)


def pick_kernel(partners_ref, in_ref, out_ref):
    for group in range(in_ref.shape[0]):
        out_ref[group, :, 0:128] = in_ref[group]
        one, two = in_ref[partners_ref[group, 0]], in_ref[partners_ref[group, 1]]
        out_ref[group, :, 128:256] = jnp.concatenate([one[:, DH:], two[:, DH:]], axis=1)


def sum_kernel(partners_ref, in_ref, out_ref, total):
    groups, sent = in_ref.shape[:2]
    for group in range(groups):
        x = in_ref[group, :, 0:128].astype(F32)
        total[group, :sent] = x
        total[group, sent:] = from_spare(x, 0, (0, 2, 3))
    left = slots(sent + REST) < 2
    for group in range(groups):
        listed = in_ref[group, :, 128:256].astype(F32)
        rest = from_spare(in_ref[group, :, 0:128].astype(F32), 3 * REST, range(4))
        listed = jnp.concatenate([listed, rest], axis=0)
        one, two = partners_ref[group, 0], partners_ref[group, 1]
        total[one] += jnp.where(left, 0.0, pltpu.roll(listed, DH, 1))
        total[two] += jnp.where(left, 0.0, listed)
    folded = out_ref.shape[1]
    for group in range(groups):
        for chunk in range(2):
            x = total[group, chunk * (folded + REST) : (chunk + 1) * (folded + REST)]
            fill = [to_spare(x[folded:], slot) for slot in (0, 2, 3)]
            fill = jnp.concatenate(fill + [jnp.zeros((folded - 3 * REST, 128), F32)], axis=0)
            out_ref[2 * group + chunk] = jnp.where(spare(folded), fill, x[:folded]).astype(BF16)


WIDE = 1152


def attend_kernel(hidden_ref, in_ref, out_ref, own, listed, kt, bias, s_ref, dp_ref, total, flat, dqt):
    sources, rows_of = in_ref.shape[:2]
    seq = own.shape[0]
    blocks = [(s // 4 * 2 + s % 2, s // 2 % 2) for s in range(sources)]
    for source, (block, half) in enumerate(blocks):
        rows = slice(block * rows_of, (block + 1) * rows_of)
        lanes = slice(128 * half, 128 * (half + 1))
        own[rows, lanes] = in_ref[source, :, 0:128]
        listed[rows, lanes] = in_ref[source, :, 128:256]
    flipped = (own[...].T, listed[...].T)
    both = lambda x, place: jnp.concatenate([x[place : place + HALF], x[128 + place : 128 + place + HALF]], axis=0)
    for j, (x, place) in enumerate(((flipped[0], DH), (flipped[1], 0), (flipped[1], DH))):
        kt[j] = both(x, place)
    flat[:DH] = (both(flipped[0], 0).astype(F32) * 0.125).astype(BF16)
    flat[DH:] = both(flipped[0], HALF)
    index = lax.broadcasted_iota(jnp.int32, bias.shape[1:], 0)
    chunk = rows_of // 2
    swap = (index >= chunk) & (index < 3 * chunk)
    place = jnp.where(swap, jnp.where(index < 2 * chunk, index + chunk, index - chunk), index)
    for j in range(2):
        bias[j] = jnp.where(place >= hidden_ref[j], 0.0, -1e30)
    total[...] = jnp.zeros_like(total)
    nt = (((1,), (1,)), ((), ()))

    def tile(start, size):
        rows = pl.ds(start, size)
        x = own[rows, :].astype(F32)
        lane = lax.broadcasted_iota(jnp.int32, x.shape, 1) % 128
        turned = jnp.concatenate([pltpu.roll(x[:, :128], DH, 1), pltpu.roll(x[:, 128:], DH, 1)], axis=1)
        q_low = jnp.where(lane < HALF, x * 0.125, 0.0).astype(BF16)
        d_low = jnp.where((lane >= HALF) & (lane < DH), x, 0.0).astype(BF16)
        q_high = jnp.where((lane >= DH) & (lane < DH + HALF), turned * 0.125, 0.0).astype(BF16)
        d_high = jnp.where(lane >= DH + HALF, turned, 0.0).astype(BF16)
        terms = ((own, q_high, d_high), (listed, q_low, d_low), (listed, q_high, d_high))
        top = jnp.full((1, size), -jnp.inf, F32)
        for j, (keys, q_side, _) in enumerate(terms):
            raw = lax.dot_general(keys[...], q_side, nt, preferred_element_type=F32)
            if j:
                head = raw[:HIDDEN_MOST] + bias[j - 1, :, :size]
                raw = jnp.concatenate([head, raw[HIDDEN_MOST:]], axis=0)
            s_ref[j, :, :size] = raw
            top = jnp.maximum(top, jnp.max(raw, axis=0, keepdims=True))
        norm = jnp.zeros((1, size), F32)
        dsum = jnp.zeros((1, size), F32)
        for j, (keys, _, d_side) in enumerate(terms):
            expo = jnp.exp(s_ref[j, :, :size] - top)
            dprod = lax.dot_general(keys[...], d_side, nt, preferred_element_type=F32)
            s_ref[j, :, :size] = expo
            dp_ref[j, :, :size] = dprod
            norm += jnp.sum(expo, axis=0, keepdims=True)
            dsum += jnp.sum(expo * dprod, axis=0, keepdims=True)
        inv = 1.0 / norm
        delta = dsum * inv
        dq = jnp.zeros((DH, size), F32)
        for j, (_, q_side, d_side) in enumerate(terms):
            prob = s_ref[j, :, :size] * inv
            dscore = (prob * (dp_ref[j, :, :size] - delta)).astype(BF16)
            total[j, :DH] += lax.dot_general(flat[:DH, rows], dscore, nt, preferred_element_type=F32)
            total[j, DH:] += lax.dot_general(flat[DH:, rows], prob.astype(BF16), nt, preferred_element_type=F32)
            dq += jnp.dot(kt[j], dscore, preferred_element_type=F32)
        dqt[:, rows] = dq

    @pl.loop(0, seq // WIDE)
    def _(i):
        tile(pl.multiple_of(i * WIDE, WIDE), WIDE)

    if seq % WIDE:
        tile(seq // WIDE * WIDE, seq % WIDE)
    gap = jnp.zeros((HALF, seq), F32)
    folded = out_ref.shape[1]
    for half in range(2):
        part = slice(HALF * half, HALF * (half + 1))
        value = slice(DH + HALF * half, DH + HALF * (half + 1))
        own_part = jnp.concatenate([dqt[part] * 0.125, gap, total[0, part], total[0, value]], axis=0).T
        listed_part = jnp.concatenate([total[1, part], total[1, value], total[2, part], total[2, value]], axis=0).T
        for source, (block, which) in enumerate(blocks):
            if which == half:
                rows = slice(block * rows_of, block * rows_of + folded)
                rest = slice(block * rows_of + folded, (block + 1) * rows_of)
                fill = [to_spare(own_part[rest], slot) for slot in (0, 2, 3)] + [to_spare(listed_part[rest], slot) for slot in range(4)]
                fill = jnp.concatenate(fill + [jnp.zeros((folded - 7 * REST, 128), F32)], axis=0)
                out_ref[source, :, 0:128] = jnp.where(spare(folded), fill, own_part[rows]).astype(BF16)
                out_ref[source, :, 128:256] = listed_part[rows].astype(BF16)


def shape(*dims):
    return jax.ShapeDtypeStruct(dims, BF16)


def attend(hidden, rows):
    seq = rows.shape[0] * rows.shape[1] // 2
    return pl.pallas_call(
        attend_kernel,
        out_shape=shape(rows.shape[0], rows.shape[1] - REST, 256),
        in_specs=[SMEM, VMEM],
        out_specs=VMEM,
        scratch_shapes=[
            pltpu.VMEM((seq, 256), BF16),
            pltpu.VMEM((seq, 256), BF16),
            pltpu.VMEM((3, DH, seq), BF16),
            pltpu.VMEM((2, HIDDEN_MOST, WIDE), F32),
            pltpu.VMEM((3, seq, WIDE), F32),
            pltpu.VMEM((3, seq, WIDE), F32),
            pltpu.VMEM((3, 2 * DH, seq), F32),
            pltpu.VMEM((2 * DH, seq), BF16),
            pltpu.VMEM((DH, seq), F32),
        ],
        compiler_params=pltpu.CompilerParams(vmem_limit_bytes=46 * 2**20),
        name="attend",
    )(hidden, rows)


def local(queries, keys_in, values_in, grad_out, partners, registers):
    rows, width = queries.shape[1:]
    groups = partners.shape[0]
    pieces = 2 * width // DH
    small = pltpu.CompilerParams(vmem_limit_bytes=32 * 2**20)
    packed = pl.pallas_call(
        pack_kernel, out_shape=shape(pieces, rows, 128), in_specs=[HBM] * 4, out_specs=VMEM, name="pack",
        compiler_params=pltpu.CompilerParams(vmem_limit_bytes=63_400_000),
        scratch_shapes=[pltpu.VMEM((rows, width), BF16)] * 4 + [pltpu.SemaphoreType.DMA((4,))],
    )(queries[0], grad_out[0], keys_in[0], values_in[0])
    by_group = lax.all_to_all(packed, OUTER, 0, 0, tiled=True).reshape(groups, 2 * rows, 128)
    picked = pl.pallas_call(
        pick_kernel, out_shape=shape(groups, 2 * rows, 256), in_specs=[SMEM, VMEM], out_specs=VMEM, name="pick", compiler_params=small
    )(partners, by_group)
    gathered = lax.all_to_all(picked, INNER, 0, 0, tiled=True)
    hidden = registers[partners[lax.axis_index(INNER)]]
    spread = lax.all_to_all(attend(hidden, gathered), INNER, 0, 0, tiled=True)
    summed = pl.pallas_call(
        sum_kernel,
        out_shape=shape(pieces, rows - REST, 128),
        in_specs=[SMEM, VMEM],
        out_specs=VMEM,
        scratch_shapes=[pltpu.VMEM((groups, 2 * rows, 128), F32)],
        name="sum",
        compiler_params=small,
    )(partners, spread)
    by_head = lax.all_to_all(summed, OUTER, 0, 0, tiled=True)
    dq, dk, dv = pl.pallas_call(
        unpack_kernel, out_shape=(shape(rows, width),) * 3, in_specs=[VMEM], out_specs=(VMEM,) * 3, name="unpack", compiler_params=small
    )(by_head)
    return dq[None], dk[None], dv[None]


def solution(mesh):
    names = tuple(name for name, _ in FINE)
    fine = Mesh(np.asarray(mesh.devices).reshape([size for _, size in FINE]), names)
    tokens = P(names[:4], names[4:], None)
    return jax.shard_map(
        local,
        mesh=fine,
        in_specs=(tokens,) * 4 + (P(), P()),
        out_specs=(tokens,) * 3,
        check_vma=False,
    )
```

```python
import jax
import jax.numpy as jnp
import numpy as np
from jax import lax
from jax.experimental import pallas as pl
from jax.experimental.pallas import tpu as pltpu
from jax.sharding import Mesh
from jax.sharding import PartitionSpec as P

DH = 64
HALF = DH // 2
REST = 16
HIDDEN_MOST = 288
BF16 = jnp.bfloat16
F32 = jnp.float32
VMEM = pl.BlockSpec(memory_space=pltpu.VMEM)
HBM = pl.BlockSpec(memory_space=pltpu.HBM)
SMEM = pl.BlockSpec(memory_space=pltpu.SMEM)

FINE = (("zh", 2), ("x1", 2), ("x0", 2), ("c", 2), ("y", 4), ("zl1", 2), ("zl0", 2))
OUTER = ("zh", "x1", "x0", "c", "zl1")
INNER = ("y", "x0", "zl0")


def piece(head, half):
    return head // 4 * 8 + half * 4 + head % 4


def columns(head, half):
    return slice(DH * head + HALF * half, DH * head + HALF * (half + 1))


def slots(rows):
    return lax.broadcasted_iota(jnp.int32, (rows, 128), 1) // HALF


def spare(rows):
    return slots(rows) == 1


def to_spare(x, slot):
    return x if slot == 1 else pltpu.roll(x, (HALF - HALF * slot) % 128, 1)


def from_spare(x, start, places):
    slot = slots(REST)
    out = jnp.zeros((REST, 128), F32)
    for i, place in enumerate(places):
        part = x[start + REST * i : start + REST * (i + 1)]
        part = part if place == 1 else pltpu.roll(part, (HALF * place - HALF) % 128, 1)
        out = jnp.where(slot == place, part, out)
    return out


def pack_kernel(q_hbm, d_hbm, k_hbm, v_hbm, out_hbm, q_ref, d_ref, k_ref, v_ref, out_ref, in_sems, out_sems):
    refs = (q_ref, d_ref, k_ref, v_ref)
    quads = q_ref.shape[1] // (4 * DH)
    fetched = []
    for quad in range(quads):
        cols = slice(4 * DH * quad, 4 * DH * (quad + 1))
        for i, (far, near) in enumerate(zip((q_hbm, d_hbm, k_hbm, v_hbm), refs)):
            fetched.append(pltpu.make_async_copy(far.at[:, cols], near.at[:, cols], in_sems.at[quad, i]))
            fetched[-1].start()
    sent = []
    for quad in range(quads):
        for copy in fetched[4 * quad : 4 * quad + 4]:
            copy.wait()
        for head in range(4 * quad, 4 * quad + 4):
            for half in range(2):
                parts = [ref[:, columns(head, half)] for ref in refs]
                out_ref[piece(head, half)] = jnp.concatenate(parts, axis=1)
        pieces = slice(8 * quad, 8 * quad + 8)
        sent.append(pltpu.make_async_copy(out_ref.at[pieces], out_hbm.at[pieces], out_sems.at[quad]))
        sent[-1].start()
    for copy in sent:
        copy.wait()


def unpack_kernel(in_ref, q_ref, k_ref, v_ref):
    def unfold(at):
        x = in_ref[at].astype(F32)
        return jnp.concatenate([x, from_spare(x, 0, (0, 2, 3))], axis=0)

    for pair in range(q_ref.shape[1] // (2 * DH)):
        parts = [unfold(piece(2 * pair + i // 2, i % 2)) for i in range(4)]
        lane = lax.broadcasted_iota(jnp.int32, parts[0].shape, 1)
        for out, place in ((q_ref, 0), (k_ref, 2), (v_ref, 3)):
            row = parts[place]
            for i in range(4):
                if i != place:
                    turned = pltpu.roll(parts[i], (HALF * (i - place)) % 128, 1)
                    row = jnp.where((lane >= HALF * i) & (lane < HALF * (i + 1)), turned, row)
            out[:, 2 * DH * pair : 2 * DH * (pair + 1)] = row.astype(BF16)


def pick_kernel(partners_ref, in_ref, out_hbm, out_ref, sems):
    sent = []
    for group in range(in_ref.shape[0]):
        out_ref[group, :, 0:128] = in_ref[group]
        one, two = in_ref[partners_ref[group, 0]], in_ref[partners_ref[group, 1]]
        out_ref[group, :, 128:256] = jnp.concatenate([one[:, DH:], two[:, DH:]], axis=1)
        sent.append(pltpu.make_async_copy(out_ref.at[group], out_hbm.at[group], sems.at[group]))
        sent[-1].start()
    for copy in sent:
        copy.wait()


def sum_kernel(partners_ref, in_ref, out_ref, total, second):
    groups, sent = in_ref.shape[:2]
    for group in range(groups):
        x = in_ref[group, :, 0:128].astype(F32)
        total[group, :sent] = x
        total[group, sent:] = from_spare(x, 0, (0, 2, 3))
    second[...] = jnp.zeros_like(second)
    left = slots(sent + REST) < 2
    for group in range(groups):
        listed = in_ref[group, :, 128:256].astype(F32)
        rest = from_spare(in_ref[group, :, 0:128].astype(F32), 3 * REST, range(4))
        listed = jnp.concatenate([listed, rest], axis=0)
        one, two = partners_ref[group, 0], partners_ref[group, 1]
        total[two] += jnp.where(left, 0.0, listed)
        second[one] += jnp.where(left, listed, 0.0)
    folded = out_ref.shape[1]
    for group in range(groups):
        for chunk in range(2):
            rows = slice(chunk * (folded + REST), (chunk + 1) * (folded + REST))
            x = total[group, rows] + pltpu.roll(second[group, rows], DH, 1)
            fill = [to_spare(x[folded:], slot) for slot in (0, 2, 3)]
            fill = jnp.concatenate(fill + [jnp.zeros((folded - 3 * REST, 128), F32)], axis=0)
            out_ref[2 * group + chunk] = jnp.where(spare(folded), fill, x[:folded]).astype(BF16)


WIDE = 1152


def attend_kernel(hidden_ref, in_ref, out_ref, own, listed, kt, bias, s_ref, dp_ref, total, flat, dqt):
    sources, rows_of = in_ref.shape[:2]
    seq = own.shape[0]
    blocks = [(s // 4 * 2 + s % 2, s // 2 % 2) for s in range(sources)]
    for source, (block, half) in enumerate(blocks):
        rows = slice(block * rows_of, (block + 1) * rows_of)
        lanes = slice(128 * half, 128 * (half + 1))
        own[rows, lanes] = in_ref[source, :, 0:128]
        listed[rows, lanes] = in_ref[source, :, 128:256]
    flipped = (own[...].T, listed[...].T)
    both = lambda x, place: jnp.concatenate([x[place : place + HALF], x[128 + place : 128 + place + HALF]], axis=0)
    for j, (x, place) in enumerate(((flipped[0], DH), (flipped[1], 0), (flipped[1], DH))):
        kt[j] = both(x, place)
    flat[:DH] = (both(flipped[0], 0).astype(F32) * 0.125).astype(BF16)
    flat[DH:] = both(flipped[0], HALF)
    index = lax.broadcasted_iota(jnp.int32, bias.shape[1:], 0)
    chunk = rows_of // 2
    swap = (index >= chunk) & (index < 3 * chunk)
    place = jnp.where(swap, jnp.where(index < 2 * chunk, index + chunk, index - chunk), index)
    for j in range(2):
        bias[j] = jnp.where(place >= hidden_ref[j], 0.0, -1e30)
    total[...] = jnp.zeros_like(total)
    nt = (((1,), (1,)), ((), ()))

    def tile(start, size):
        rows = pl.ds(start, size)
        x = own[rows, :].astype(F32)
        lane = lax.broadcasted_iota(jnp.int32, x.shape, 1) % 128
        turned = jnp.concatenate([pltpu.roll(x[:, :128], DH, 1), pltpu.roll(x[:, 128:], DH, 1)], axis=1)
        q_low = jnp.where(lane < HALF, x * 0.125, 0.0).astype(BF16)
        d_low = jnp.where((lane >= HALF) & (lane < DH), x, 0.0).astype(BF16)
        q_high = jnp.where((lane >= DH) & (lane < DH + HALF), turned * 0.125, 0.0).astype(BF16)
        d_high = jnp.where(lane >= DH + HALF, turned, 0.0).astype(BF16)
        terms = ((own, q_high, d_high), (listed, q_low, d_low), (listed, q_high, d_high))
        top = jnp.full((1, size), -jnp.inf, F32)
        for j, (keys, q_side, _) in enumerate(terms):
            raw = lax.dot_general(keys[...], q_side, nt, preferred_element_type=F32)
            if j:
                head = raw[:HIDDEN_MOST] + jnp.concatenate([bias[j - 1]] * (size // 128), axis=1)
                raw = jnp.concatenate([head, raw[HIDDEN_MOST:]], axis=0)
            s_ref[j, :, :size] = raw
            top = jnp.maximum(top, jnp.max(raw, axis=0, keepdims=True))
        norm = jnp.zeros((1, size), F32)
        dsum = jnp.zeros((1, size), F32)
        for j, (keys, _, d_side) in enumerate(terms):
            expo = jnp.exp(s_ref[j, :, :size] - top)
            dprod = lax.dot_general(keys[...], d_side, nt, preferred_element_type=F32)
            s_ref[j, :, :size] = expo
            dp_ref[j, :, :size] = dprod
            norm += jnp.sum(expo, axis=0, keepdims=True)
            dsum += jnp.sum(expo * dprod, axis=0, keepdims=True)
        inv = 1.0 / norm
        delta = dsum * inv
        dq = jnp.zeros((DH, size), F32)
        for j, (_, q_side, d_side) in enumerate(terms):
            prob = s_ref[j, :, :size] * inv
            dscore = (prob * (dp_ref[j, :, :size] - delta)).astype(BF16)
            total[j, :DH] += lax.dot_general(flat[:DH, rows], dscore, nt, preferred_element_type=F32)
            total[j, DH:] += lax.dot_general(flat[DH:, rows], prob.astype(BF16), nt, preferred_element_type=F32)
            dq += jnp.dot(kt[j], dscore, preferred_element_type=F32)
        dqt[:, rows] = dq

    @pl.loop(0, seq // WIDE)
    def _(i):
        tile(pl.multiple_of(i * WIDE, WIDE), WIDE)

    if seq % WIDE:
        tile(seq // WIDE * WIDE, seq % WIDE)
    gap = jnp.zeros((HALF, seq), F32)
    folded = out_ref.shape[1]
    for half in range(2):
        part = slice(HALF * half, HALF * (half + 1))
        value = slice(DH + HALF * half, DH + HALF * (half + 1))
        own_part = jnp.concatenate([dqt[part] * 0.125, gap, total[0, part], total[0, value]], axis=0).T
        listed_part = jnp.concatenate([total[1, part], total[1, value], total[2, part], total[2, value]], axis=0).T
        for source, (block, which) in enumerate(blocks):
            if which == half:
                rows = slice(block * rows_of, block * rows_of + folded)
                rest = slice(block * rows_of + folded, (block + 1) * rows_of)
                fill = [to_spare(own_part[rest], slot) for slot in (0, 2, 3)] + [to_spare(listed_part[rest], slot) for slot in range(4)]
                fill = jnp.concatenate(fill + [jnp.zeros((folded - 7 * REST, 128), F32)], axis=0)
                out_ref[source, :, 0:128] = jnp.where(spare(folded), fill, own_part[rows]).astype(BF16)
                out_ref[source, :, 128:256] = listed_part[rows].astype(BF16)


def shape(*dims):
    return jax.ShapeDtypeStruct(dims, BF16)


def attend(hidden, rows):
    seq = rows.shape[0] * rows.shape[1] // 2
    return pl.pallas_call(
        attend_kernel,
        out_shape=shape(rows.shape[0], rows.shape[1] - REST, 256),
        in_specs=[SMEM, VMEM],
        out_specs=VMEM,
        scratch_shapes=[
            pltpu.VMEM((seq, 256), BF16),
            pltpu.VMEM((seq, 256), BF16),
            pltpu.VMEM((3, DH, seq), BF16),
            pltpu.VMEM((2, HIDDEN_MOST, 128), F32),
            pltpu.VMEM((3, seq, WIDE), F32),
            pltpu.VMEM((3, seq, WIDE), F32),
            pltpu.VMEM((3, 2 * DH, seq), F32),
            pltpu.VMEM((2 * DH, seq), BF16),
            pltpu.VMEM((DH, seq), F32),
        ],
        compiler_params=pltpu.CompilerParams(vmem_limit_bytes=46 * 2**20),
        name="attend",
    )(hidden, rows)


def local(queries, keys_in, values_in, grad_out, partners, registers):
    rows, width = queries.shape[1:]
    groups = partners.shape[0]
    pieces = 2 * width // DH
    small = pltpu.CompilerParams(vmem_limit_bytes=32 * 2**20)
    packed = pl.pallas_call(
        pack_kernel,
        out_shape=shape(pieces, rows, 128),
        in_specs=[HBM] * 4,
        out_specs=HBM,
        scratch_shapes=[pltpu.VMEM((rows, width), BF16)] * 4
        + [
            pltpu.VMEM((pieces, rows, 128), BF16),
            pltpu.SemaphoreType.DMA((pieces // 8, 4)),
            pltpu.SemaphoreType.DMA((pieces // 8,)),
        ],
        name="pack",
        compiler_params=pltpu.CompilerParams(vmem_limit_bytes=63_400_000),
    )(queries[0], grad_out[0], keys_in[0], values_in[0])
    by_group = lax.all_to_all(packed, OUTER, 0, 0, tiled=True).reshape(groups, 2 * rows, 128)
    picked = pl.pallas_call(
        pick_kernel,
        out_shape=shape(groups, 2 * rows, 256),
        in_specs=[SMEM, VMEM],
        out_specs=HBM,
        scratch_shapes=[pltpu.VMEM((groups, 2 * rows, 256), BF16), pltpu.SemaphoreType.DMA((groups,))],
        name="pick",
        compiler_params=small,
    )(partners, by_group)
    gathered = lax.all_to_all(picked, INNER, 0, 0, tiled=True)
    hidden = registers[partners[lax.axis_index(INNER)]]
    spread = lax.all_to_all(attend(hidden, gathered), INNER, 0, 0, tiled=True)
    summed = pl.pallas_call(
        sum_kernel,
        out_shape=shape(pieces, rows - REST, 128),
        in_specs=[SMEM, VMEM],
        out_specs=VMEM,
        scratch_shapes=[pltpu.VMEM((groups, 2 * rows, 128), F32)] * 2,
        name="sum",
        compiler_params=small,
    )(partners, spread)
    by_head = lax.all_to_all(summed, OUTER, 0, 0, tiled=True)
    dq, dk, dv = pl.pallas_call(
        unpack_kernel, out_shape=(shape(rows, width),) * 3, in_specs=[VMEM], out_specs=(VMEM,) * 3, name="unpack", compiler_params=small
    )(by_head)
    return dq[None], dk[None], dv[None]


def solution(mesh):
    names = tuple(name for name, _ in FINE)
    fine = Mesh(np.asarray(mesh.devices).reshape([size for _, size in FINE]), names)
    tokens = P(names[:4], names[4:], None)
    return jax.shard_map(
        local,
        mesh=fine,
        in_specs=(tokens,) * 4 + (P(), P()),
        out_specs=(tokens,) * 3,
        check_vma=False,
    )
```

```python
import jax
import jax.numpy as jnp
import numpy as np
from jax import lax
from jax.experimental import pallas as pl
from jax.experimental.pallas import tpu as pltpu
from jax.sharding import Mesh
from jax.sharding import PartitionSpec as P

DH = 64
HALF = DH // 2
REST = 16
HIDDEN_MOST = 288
BF16 = jnp.bfloat16
F32 = jnp.float32
VMEM = pl.BlockSpec(memory_space=pltpu.VMEM)
HBM = pl.BlockSpec(memory_space=pltpu.HBM)
SMEM = pl.BlockSpec(memory_space=pltpu.SMEM)

FINE = (("zh", 2), ("x1", 2), ("x0", 2), ("c", 2), ("y", 4), ("zl1", 2), ("zl0", 2))
OUTER = ("zl1", "zh", "x1", "x0", "c")
INNER = ("x0", "y", "zl0")


def piece(head, half):
    return head // 2 * 4 + half * 2 + head % 2


def columns(head, half):
    return slice(DH * head + HALF * half, DH * head + HALF * (half + 1))


def slots(rows):
    return lax.broadcasted_iota(jnp.int32, (rows, 128), 1) // HALF


def spare(rows):
    return slots(rows) == 1


def to_spare(x, slot):
    return x if slot == 1 else pltpu.roll(x, (HALF - HALF * slot) % 128, 1)


def from_spare(x, start, places):
    slot = slots(REST)
    out = jnp.zeros((REST, 128), F32)
    for i, place in enumerate(places):
        part = x[start + REST * i : start + REST * (i + 1)]
        part = part if place == 1 else pltpu.roll(part, (HALF * place - HALF) % 128, 1)
        out = jnp.where(slot == place, part, out)
    return out


def pack_kernel(q_hbm, d_hbm, k_hbm, v_hbm, out_ref, q_ref, d_ref, k_ref, v_ref, sems):
    refs = (q_ref, d_ref, k_ref, v_ref)
    copies = [pltpu.make_async_copy(a, b, sems.at[i]) for i, (a, b) in enumerate(zip((q_hbm, d_hbm, k_hbm, v_hbm), refs))]
    for copy in copies:
        copy.start()
    for copy in copies:
        copy.wait()
    for head in range(q_ref.shape[1] // DH):
        for half in range(2):
            parts = [ref[:, columns(head, half)] for ref in refs]
            out_ref[piece(head, half)] = jnp.concatenate(parts, axis=1)


def unpack_kernel(in_ref, q_ref, k_ref, v_ref):
    def unfold(at):
        x = in_ref[at].astype(F32)
        return jnp.concatenate([x, from_spare(x, 0, (0, 2, 3))], axis=0)

    for pair in range(q_ref.shape[1] // (2 * DH)):
        parts = [unfold(piece(2 * pair + i // 2, i % 2)) for i in range(4)]
        lane = lax.broadcasted_iota(jnp.int32, parts[0].shape, 1)
        for out, place in ((q_ref, 0), (k_ref, 2), (v_ref, 3)):
            row = parts[place]
            for i in range(4):
                if i != place:
                    turned = pltpu.roll(parts[i], (HALF * (i - place)) % 128, 1)
                    row = jnp.where((lane >= HALF * i) & (lane < HALF * (i + 1)), turned, row)
            out[:, 2 * DH * pair : 2 * DH * (pair + 1)] = row.astype(BF16)


def pick_kernel(partners_ref, in_ref, out_ref):
    groups, chunks = out_ref.shape[:2]
    for group in range(groups):
        for chunk in range(chunks):
            first = chunk * groups
            out_ref[group, chunk, :, 0:128] = in_ref[first + group]
            one, two = (in_ref[first + partners_ref[group, slot]] for slot in range(2))
            out_ref[group, chunk, :, 128:256] = jnp.concatenate([one[:, DH:], two[:, DH:]], axis=1)


def sum_kernel(partners_ref, in_ref, out_ref, total):
    groups, sent = in_ref.shape[:2]
    for group in range(groups):
        x = in_ref[group, :, 0:128].astype(F32)
        total[group, :sent] = x
        total[group, sent:] = from_spare(x, 0, (0, 2, 3))
    left = slots(sent + REST) < 2
    for group in range(groups):
        listed = in_ref[group, :, 128:256].astype(F32)
        rest = from_spare(in_ref[group, :, 0:128].astype(F32), 3 * REST, range(4))
        listed = jnp.concatenate([listed, rest], axis=0)
        one, two = partners_ref[group, 0], partners_ref[group, 1]
        total[one] += jnp.where(left, 0.0, pltpu.roll(listed, DH, 1))
        total[two] += jnp.where(left, 0.0, listed)
    folded = out_ref.shape[1]
    for group in range(groups):
        for chunk in range(2):
            x = total[group, chunk * (folded + REST) : (chunk + 1) * (folded + REST)]
            fill = [to_spare(x[folded:], slot) for slot in (0, 2, 3)]
            fill = jnp.concatenate(fill + [jnp.zeros((folded - 3 * REST, 128), F32)], axis=0)
            out_ref[chunk * groups + group] = jnp.where(spare(folded), fill, x[:folded]).astype(BF16)


WIDE = 1152


def attend_kernel(hidden_ref, in_ref, out_ref, own, listed, kt, bias, s_ref, dp_ref, total, flat, dqt):
    sources, rows_of = in_ref.shape[:2]
    seq = own.shape[0]
    blocks = [(s % (sources // 2), s // (sources // 2)) for s in range(sources)]
    for source, (block, half) in enumerate(blocks):
        rows = slice(block * rows_of, (block + 1) * rows_of)
        lanes = slice(128 * half, 128 * (half + 1))
        own[rows, lanes] = in_ref[source, :, 0:128]
        listed[rows, lanes] = in_ref[source, :, 128:256]
    flipped = (own[...].T, listed[...].T)
    both = lambda x, place: jnp.concatenate([x[place : place + HALF], x[128 + place : 128 + place + HALF]], axis=0)
    for j, (x, place) in enumerate(((flipped[0], DH), (flipped[1], 0), (flipped[1], DH))):
        kt[j] = both(x, place)
    flat[:DH] = (both(flipped[0], 0).astype(F32) * 0.125).astype(BF16)
    flat[DH:] = both(flipped[0], HALF)
    index = lax.broadcasted_iota(jnp.int32, bias.shape[1:], 0)
    chunk = rows_of // 2
    swap = (index >= chunk) & (index < 3 * chunk)
    place = jnp.where(swap, jnp.where(index < 2 * chunk, index + chunk, index - chunk), index)
    for j in range(2):
        bias[j] = jnp.where(place >= hidden_ref[j], 0.0, -1e30)
    total[...] = jnp.zeros_like(total)
    nt = (((1,), (1,)), ((), ()))

    def tile(start, size):
        rows = pl.ds(start, size)
        x = own[rows, :].astype(F32)
        lane = lax.broadcasted_iota(jnp.int32, x.shape, 1) % 128
        turned = jnp.concatenate([pltpu.roll(x[:, :128], DH, 1), pltpu.roll(x[:, 128:], DH, 1)], axis=1)
        q_low = jnp.where(lane < HALF, x * 0.125, 0.0).astype(BF16)
        d_low = jnp.where((lane >= HALF) & (lane < DH), x, 0.0).astype(BF16)
        q_high = jnp.where((lane >= DH) & (lane < DH + HALF), turned * 0.125, 0.0).astype(BF16)
        d_high = jnp.where(lane >= DH + HALF, turned, 0.0).astype(BF16)
        terms = ((own, q_high, d_high), (listed, q_low, d_low), (listed, q_high, d_high))
        top = jnp.full((1, size), -jnp.inf, F32)
        for j, (keys, q_side, _) in enumerate(terms):
            raw = lax.dot_general(keys[...], q_side, nt, preferred_element_type=F32)
            if j:
                head = raw[:HIDDEN_MOST] + bias[j - 1, :, :size]
                raw = jnp.concatenate([head, raw[HIDDEN_MOST:]], axis=0)
            s_ref[j, :, :size] = raw
            top = jnp.maximum(top, jnp.max(raw, axis=0, keepdims=True))
        norm = jnp.zeros((1, size), F32)
        dsum = jnp.zeros((1, size), F32)
        for j, (keys, _, d_side) in enumerate(terms):
            expo = jnp.exp(s_ref[j, :, :size] - top)
            dprod = lax.dot_general(keys[...], d_side, nt, preferred_element_type=F32)
            s_ref[j, :, :size] = expo
            dp_ref[j, :, :size] = dprod
            norm += jnp.sum(expo, axis=0, keepdims=True)
            dsum += jnp.sum(expo * dprod, axis=0, keepdims=True)
        inv = 1.0 / norm
        delta = dsum * inv
        dq = jnp.zeros((DH, size), F32)
        for j, (_, q_side, d_side) in enumerate(terms):
            prob = s_ref[j, :, :size] * inv
            dscore = (prob * (dp_ref[j, :, :size] - delta)).astype(BF16)
            total[j, :DH] += lax.dot_general(flat[:DH, rows], dscore, nt, preferred_element_type=F32)
            total[j, DH:] += lax.dot_general(flat[DH:, rows], prob.astype(BF16), nt, preferred_element_type=F32)
            dq += jnp.dot(kt[j], dscore, preferred_element_type=F32)
        dqt[:, rows] = dq

    @pl.loop(0, seq // WIDE)
    def _(i):
        tile(pl.multiple_of(i * WIDE, WIDE), WIDE)

    if seq % WIDE:
        tile(seq // WIDE * WIDE, seq % WIDE)
    gap = jnp.zeros((HALF, seq), F32)
    folded = out_ref.shape[1]
    for half in range(2):
        part = slice(HALF * half, HALF * (half + 1))
        value = slice(DH + HALF * half, DH + HALF * (half + 1))
        own_part = jnp.concatenate([dqt[part] * 0.125, gap, total[0, part], total[0, value]], axis=0).T
        listed_part = jnp.concatenate([total[1, part], total[1, value], total[2, part], total[2, value]], axis=0).T
        for source, (block, which) in enumerate(blocks):
            if which == half:
                rows = slice(block * rows_of, block * rows_of + folded)
                rest = slice(block * rows_of + folded, (block + 1) * rows_of)
                fill = [to_spare(own_part[rest], slot) for slot in (0, 2, 3)] + [to_spare(listed_part[rest], slot) for slot in range(4)]
                fill = jnp.concatenate(fill + [jnp.zeros((folded - 7 * REST, 128), F32)], axis=0)
                out_ref[source, :, 0:128] = jnp.where(spare(folded), fill, own_part[rows]).astype(BF16)
                out_ref[source, :, 128:256] = listed_part[rows].astype(BF16)


def shape(*dims):
    return jax.ShapeDtypeStruct(dims, BF16)


def attend(hidden, rows):
    seq = rows.shape[0] * rows.shape[1] // 2
    return pl.pallas_call(
        attend_kernel,
        out_shape=shape(rows.shape[0], rows.shape[1] - REST, 256),
        in_specs=[SMEM, VMEM],
        out_specs=VMEM,
        scratch_shapes=[
            pltpu.VMEM((seq, 256), BF16),
            pltpu.VMEM((seq, 256), BF16),
            pltpu.VMEM((3, DH, seq), BF16),
            pltpu.VMEM((2, HIDDEN_MOST, WIDE), F32),
            pltpu.VMEM((3, seq, WIDE), F32),
            pltpu.VMEM((3, seq, WIDE), F32),
            pltpu.VMEM((3, 2 * DH, seq), F32),
            pltpu.VMEM((2 * DH, seq), BF16),
            pltpu.VMEM((DH, seq), F32),
        ],
        compiler_params=pltpu.CompilerParams(vmem_limit_bytes=46 * 2**20),
        name="attend",
    )(hidden, rows)


def local(queries, keys_in, values_in, grad_out, partners, registers):
    rows, width = queries.shape[1:]
    groups = partners.shape[0]
    pieces = 2 * width // DH
    small = pltpu.CompilerParams(vmem_limit_bytes=32 * 2**20)
    packed = pl.pallas_call(
        pack_kernel, out_shape=shape(pieces, rows, 128), in_specs=[HBM] * 4, out_specs=VMEM, name="pack",
        compiler_params=pltpu.CompilerParams(vmem_limit_bytes=63_400_000),
        scratch_shapes=[pltpu.VMEM((rows, width), BF16)] * 4 + [pltpu.SemaphoreType.DMA((4,))],
    )(queries[0], grad_out[0], keys_in[0], values_in[0])
    by_group = lax.all_to_all(packed, OUTER, 0, 0, tiled=True)
    picked = pl.pallas_call(
        pick_kernel, out_shape=shape(groups, 2, rows, 256), in_specs=[SMEM, VMEM], out_specs=VMEM, name="pick", compiler_params=small
    )(partners, by_group)
    gathered = lax.all_to_all(picked.reshape(groups, 2 * rows, 256), INNER, 0, 0, tiled=True)
    hidden = registers[partners[lax.axis_index(INNER)]]
    spread = lax.all_to_all(attend(hidden, gathered), INNER, 0, 0, tiled=True)
    summed = pl.pallas_call(
        sum_kernel,
        out_shape=shape(pieces, rows - REST, 128),
        in_specs=[SMEM, VMEM],
        out_specs=VMEM,
        scratch_shapes=[pltpu.VMEM((groups, 2 * rows, 128), F32)],
        name="sum",
        compiler_params=small,
    )(partners, spread)
    by_head = lax.all_to_all(summed, OUTER, 0, 0, tiled=True)
    dq, dk, dv = pl.pallas_call(
        unpack_kernel, out_shape=(shape(rows, width),) * 3, in_specs=[VMEM], out_specs=(VMEM,) * 3, name="unpack", compiler_params=small
    )(by_head)
    return dq[None], dk[None], dv[None]


def solution(mesh):
    names = tuple(name for name, _ in FINE)
    fine = Mesh(np.asarray(mesh.devices).reshape([size for _, size in FINE]), names)
    tokens = P(names[:4], names[4:], None)
    return jax.shard_map(
        local,
        mesh=fine,
        in_specs=(tokens,) * 4 + (P(), P()),
        out_specs=(tokens,) * 3,
        check_vma=False,
    )
```

```python
import jax
import jax.numpy as jnp
import numpy as np
from jax import lax
from jax.experimental import pallas as pl
from jax.experimental.pallas import tpu as pltpu
from jax.sharding import Mesh
from jax.sharding import PartitionSpec as P

DH = 64
HALF = DH // 2
REST = 16
HIDDEN_MOST = 288
BF16 = jnp.bfloat16
F32 = jnp.float32
VMEM = pl.BlockSpec(memory_space=pltpu.VMEM)
HBM = pl.BlockSpec(memory_space=pltpu.HBM)
SMEM = pl.BlockSpec(memory_space=pltpu.SMEM)

FINE = (("zh", 2), ("x1", 2), ("x0", 2), ("c", 2), ("y", 4), ("zl1", 2), ("zl0", 2))
OUTER = ("zl1", "zh", "x1", "x0", "c")
INNER = ("y", "x0", "zl0")


def piece(head, half):
    return head // 2 * 4 + half * 2 + head % 2


def columns(head, half):
    return slice(DH * head + HALF * half, DH * head + HALF * (half + 1))


def slots(rows):
    return lax.broadcasted_iota(jnp.int32, (rows, 128), 1) // HALF


def spare(rows):
    return slots(rows) == 1


def to_spare(x, slot):
    return x if slot == 1 else pltpu.roll(x, (HALF - HALF * slot) % 128, 1)


def from_spare(x, start, places):
    slot = slots(REST)
    out = jnp.zeros((REST, 128), F32)
    for i, place in enumerate(places):
        part = x[start + REST * i : start + REST * (i + 1)]
        part = part if place == 1 else pltpu.roll(part, (HALF * place - HALF) % 128, 1)
        out = jnp.where(slot == place, part, out)
    return out


def pack_kernel(q_hbm, d_hbm, k_hbm, v_hbm, out_ref, q_ref, d_ref, k_ref, v_ref, sems):
    refs = (q_ref, d_ref, k_ref, v_ref)
    copies = [pltpu.make_async_copy(a, b, sems.at[i]) for i, (a, b) in enumerate(zip((q_hbm, d_hbm, k_hbm, v_hbm), refs))]
    for copy in copies:
        copy.start()
    for copy in copies:
        copy.wait()
    for head in range(q_ref.shape[1] // DH):
        for half in range(2):
            parts = [ref[:, columns(head, half)] for ref in refs]
            out_ref[piece(head, half)] = jnp.concatenate(parts, axis=1)


def unpack_kernel(in_ref, q_ref, k_ref, v_ref):
    def unfold(at):
        x = in_ref[at].astype(F32)
        return jnp.concatenate([x, from_spare(x, 0, (0, 2, 3))], axis=0)

    for pair in range(q_ref.shape[1] // (2 * DH)):
        parts = [unfold(piece(2 * pair + i // 2, i % 2)) for i in range(4)]
        lane = lax.broadcasted_iota(jnp.int32, parts[0].shape, 1)
        for out, place in ((q_ref, 0), (k_ref, 2), (v_ref, 3)):
            row = parts[place]
            for i in range(4):
                if i != place:
                    turned = pltpu.roll(parts[i], (HALF * (i - place)) % 128, 1)
                    row = jnp.where((lane >= HALF * i) & (lane < HALF * (i + 1)), turned, row)
            out[:, 2 * DH * pair : 2 * DH * (pair + 1)] = row.astype(BF16)


def pick_kernel(partners_ref, in_ref, out_ref):
    groups, chunks = out_ref.shape[:2]
    for group in range(groups):
        for chunk in range(chunks):
            first = chunk * groups
            out_ref[group, chunk, :, 0:128] = in_ref[first + group]
            one, two = (in_ref[first + partners_ref[group, slot]] for slot in range(2))
            out_ref[group, chunk, :, 128:256] = jnp.concatenate([one[:, DH:], two[:, DH:]], axis=1)


def sum_kernel(partners_ref, in_ref, out_ref, total):
    groups, sent = in_ref.shape[:2]
    for group in range(groups):
        x = in_ref[group, :, 0:128].astype(F32)
        total[group, :sent] = x
        total[group, sent:] = from_spare(x, 0, (0, 2, 3))
    left = slots(sent + REST) < 2
    for group in range(groups):
        listed = in_ref[group, :, 128:256].astype(F32)
        rest = from_spare(in_ref[group, :, 0:128].astype(F32), 3 * REST, range(4))
        listed = jnp.concatenate([listed, rest], axis=0)
        one, two = partners_ref[group, 0], partners_ref[group, 1]
        total[one] += jnp.where(left, 0.0, pltpu.roll(listed, DH, 1))
        total[two] += jnp.where(left, 0.0, listed)
    folded = out_ref.shape[1]
    for group in range(groups):
        for chunk in range(2):
            x = total[group, chunk * (folded + REST) : (chunk + 1) * (folded + REST)]
            fill = [to_spare(x[folded:], slot) for slot in (0, 2, 3)]
            fill = jnp.concatenate(fill + [jnp.zeros((folded - 3 * REST, 128), F32)], axis=0)
            out_ref[chunk * groups + group] = jnp.where(spare(folded), fill, x[:folded]).astype(BF16)


WIDE = 1152


def attend_kernel(hidden_ref, in_ref, out_ref, own, listed, kt, bias, s_ref, dp_ref, total, flat, dqt):
    sources, rows_of = in_ref.shape[:2]
    seq = own.shape[0]
    blocks = [(s // 4 * 2 + s % 2, s // 2 % 2) for s in range(sources)]
    for source, (block, half) in enumerate(blocks):
        rows = slice(block * rows_of, (block + 1) * rows_of)
        lanes = slice(128 * half, 128 * (half + 1))
        own[rows, lanes] = in_ref[source, :, 0:128]
        listed[rows, lanes] = in_ref[source, :, 128:256]
    flipped = (own[...].T, listed[...].T)
    both = lambda x, place: jnp.concatenate([x[place : place + HALF], x[128 + place : 128 + place + HALF]], axis=0)
    for j, (x, place) in enumerate(((flipped[0], DH), (flipped[1], 0), (flipped[1], DH))):
        kt[j] = both(x, place)
    flat[:DH] = (both(flipped[0], 0).astype(F32) * 0.125).astype(BF16)
    flat[DH:] = both(flipped[0], HALF)
    index = lax.broadcasted_iota(jnp.int32, bias.shape[1:], 0)
    chunk = rows_of // 2
    swap = (index >= chunk) & (index < 3 * chunk)
    place = jnp.where(swap, jnp.where(index < 2 * chunk, index + chunk, index - chunk), index)
    for j in range(2):
        bias[j] = jnp.where(place >= hidden_ref[j], 0.0, -1e30)
    total[...] = jnp.zeros_like(total)
    nt = (((1,), (1,)), ((), ()))

    def tile(start, size):
        rows = pl.ds(start, size)
        x = own[rows, :].astype(F32)
        lane = lax.broadcasted_iota(jnp.int32, x.shape, 1) % 128
        turned = jnp.concatenate([pltpu.roll(x[:, :128], DH, 1), pltpu.roll(x[:, 128:], DH, 1)], axis=1)
        q_low = jnp.where(lane < HALF, x * 0.125, 0.0).astype(BF16)
        d_low = jnp.where((lane >= HALF) & (lane < DH), x, 0.0).astype(BF16)
        q_high = jnp.where((lane >= DH) & (lane < DH + HALF), turned * 0.125, 0.0).astype(BF16)
        d_high = jnp.where(lane >= DH + HALF, turned, 0.0).astype(BF16)
        terms = ((own, q_high, d_high), (listed, q_low, d_low), (listed, q_high, d_high))
        top = jnp.full((1, size), -jnp.inf, F32)
        for j, (keys, q_side, _) in enumerate(terms):
            raw = lax.dot_general(keys[...], q_side, nt, preferred_element_type=F32)
            if j:
                head = raw[:HIDDEN_MOST] + bias[j - 1, :, :size]
                raw = jnp.concatenate([head, raw[HIDDEN_MOST:]], axis=0)
            s_ref[j, :, :size] = raw
            top = jnp.maximum(top, jnp.max(raw, axis=0, keepdims=True))
        norm = jnp.zeros((1, size), F32)
        dsum = jnp.zeros((1, size), F32)
        for j, (keys, _, d_side) in enumerate(terms):
            expo = jnp.exp(s_ref[j, :, :size] - top)
            dprod = lax.dot_general(keys[...], d_side, nt, preferred_element_type=F32)
            s_ref[j, :, :size] = expo
            dp_ref[j, :, :size] = dprod
            norm += jnp.sum(expo, axis=0, keepdims=True)
            dsum += jnp.sum(expo * dprod, axis=0, keepdims=True)
        inv = 1.0 / norm
        delta = dsum * inv
        dq = jnp.zeros((DH, size), F32)
        for j, (_, q_side, d_side) in enumerate(terms):
            prob = s_ref[j, :, :size] * inv
            dscore = (prob * (dp_ref[j, :, :size] - delta)).astype(BF16)
            total[j, :DH] += lax.dot_general(flat[:DH, rows], dscore, nt, preferred_element_type=F32)
            total[j, DH:] += lax.dot_general(flat[DH:, rows], prob.astype(BF16), nt, preferred_element_type=F32)
            dq += jnp.dot(kt[j], dscore, preferred_element_type=F32)
        dqt[:, rows] = dq

    @pl.loop(0, seq // WIDE)
    def _(i):
        tile(pl.multiple_of(i * WIDE, WIDE), WIDE)

    if seq % WIDE:
        tile(seq // WIDE * WIDE, seq % WIDE)
    gap = jnp.zeros((HALF, seq), F32)
    folded = out_ref.shape[1]
    for half in range(2):
        part = slice(HALF * half, HALF * (half + 1))
        value = slice(DH + HALF * half, DH + HALF * (half + 1))
        own_part = jnp.concatenate([dqt[part] * 0.125, gap, total[0, part], total[0, value]], axis=0).T
        listed_part = jnp.concatenate([total[1, part], total[1, value], total[2, part], total[2, value]], axis=0).T
        for source, (block, which) in enumerate(blocks):
            if which == half:
                rows = slice(block * rows_of, block * rows_of + folded)
                rest = slice(block * rows_of + folded, (block + 1) * rows_of)
                fill = [to_spare(own_part[rest], slot) for slot in (0, 2, 3)] + [to_spare(listed_part[rest], slot) for slot in range(4)]
                fill = jnp.concatenate(fill + [jnp.zeros((folded - 7 * REST, 128), F32)], axis=0)
                out_ref[source, :, 0:128] = jnp.where(spare(folded), fill, own_part[rows]).astype(BF16)
                out_ref[source, :, 128:256] = listed_part[rows].astype(BF16)


def shape(*dims):
    return jax.ShapeDtypeStruct(dims, BF16)


def attend(hidden, rows):
    seq = rows.shape[0] * rows.shape[1] // 2
    return pl.pallas_call(
        attend_kernel,
        out_shape=shape(rows.shape[0], rows.shape[1] - REST, 256),
        in_specs=[SMEM, VMEM],
        out_specs=VMEM,
        scratch_shapes=[
            pltpu.VMEM((seq, 256), BF16),
            pltpu.VMEM((seq, 256), BF16),
            pltpu.VMEM((3, DH, seq), BF16),
            pltpu.VMEM((2, HIDDEN_MOST, WIDE), F32),
            pltpu.VMEM((3, seq, WIDE), F32),
            pltpu.VMEM((3, seq, WIDE), F32),
            pltpu.VMEM((3, 2 * DH, seq), F32),
            pltpu.VMEM((2 * DH, seq), BF16),
            pltpu.VMEM((DH, seq), F32),
        ],
        compiler_params=pltpu.CompilerParams(vmem_limit_bytes=46 * 2**20),
        name="attend",
    )(hidden, rows)


def local(queries, keys_in, values_in, grad_out, partners, registers):
    rows, width = queries.shape[1:]
    groups = partners.shape[0]
    pieces = 2 * width // DH
    small = pltpu.CompilerParams(vmem_limit_bytes=32 * 2**20)
    packed = pl.pallas_call(
        pack_kernel, out_shape=shape(pieces, rows, 128), in_specs=[HBM] * 4, out_specs=VMEM, name="pack",
        compiler_params=pltpu.CompilerParams(vmem_limit_bytes=63_400_000),
        scratch_shapes=[pltpu.VMEM((rows, width), BF16)] * 4 + [pltpu.SemaphoreType.DMA((4,))],
    )(queries[0], grad_out[0], keys_in[0], values_in[0])
    by_group = lax.all_to_all(packed, OUTER, 0, 0, tiled=True)
    picked = pl.pallas_call(
        pick_kernel, out_shape=shape(groups, 2, rows, 256), in_specs=[SMEM, VMEM], out_specs=VMEM, name="pick", compiler_params=small
    )(partners, by_group)
    gathered = lax.all_to_all(picked.reshape(groups, 2 * rows, 256), INNER, 0, 0, tiled=True)
    hidden = registers[partners[lax.axis_index(INNER)]]
    spread = lax.all_to_all(attend(hidden, gathered), INNER, 0, 0, tiled=True)
    summed = pl.pallas_call(
        sum_kernel,
        out_shape=shape(pieces, rows - REST, 128),
        in_specs=[SMEM, VMEM],
        out_specs=VMEM,
        scratch_shapes=[pltpu.VMEM((groups, 2 * rows, 128), F32)],
        name="sum",
        compiler_params=small,
    )(partners, spread)
    by_head = lax.all_to_all(summed, OUTER, 0, 0, tiled=True)
    dq, dk, dv = pl.pallas_call(
        unpack_kernel, out_shape=(shape(rows, width),) * 3, in_specs=[VMEM], out_specs=(VMEM,) * 3, name="unpack", compiler_params=small
    )(by_head)
    return dq[None], dk[None], dv[None]


def solution(mesh):
    names = tuple(name for name, _ in FINE)
    fine = Mesh(np.asarray(mesh.devices).reshape([size for _, size in FINE]), names)
    tokens = P(names[:4], names[4:], None)
    return jax.shard_map(
        local,
        mesh=fine,
        in_specs=(tokens,) * 4 + (P(), P()),
        out_specs=(tokens,) * 3,
        check_vma=False,
    )
```
